32 devices in a mesh: gx: 8 (over y, x, core), ba: 4 (over z).
Axes of the slice: x: 2, y: 2, z: 4, core: 2. Of those that a mesh axis runs over, the one named last changes fastest.
Arguments:
- phi_start: float32 [64, 16, 256, 256], P('gx', 'ba'), may hold values from -6 to 6
- coeff: float32 [64, 256, 256], P('gx'), may hold values from 1 to 3
- forward: float32 [2, 2, 64, 256, 256], P(None, None, None, 'gx'), may hold values from -6 to 6
- rates: float32 [16], P('ba'), may hold values from 0.02 to 0.2
- speeds: float32 [16], P('ba'), may hold values from 0.5 to 2
- shares: float32 [16], P('ba'), may hold values from 0.02 to 0.12
Outputs:
- phi_out: float32 [64, 16, 256, 256], P('gx', 'ba')
- grad: float32 [64, 12, 16], P('gx', None, 'ba')
The draws below stay inside these ranges and needn't reach their ends.
All inputs are finite; a program needn't handle non-finite values.
Results may differ from the reference program's by a relative error of at most 0.00026.
Values sent between devices are 32-bit elements; how exact they have to be, the bound alone decides.
No kernel may reach another device: no remote copies, remote signals or barrier semaphores. Data moves between devices by JAX's collectives and lax.ppermute only.
A program may use at most 192 MiB of HBM per device.

```python
import math
import jax
import jax.numpy as jnp
from jax import lax

NX = 256
NY = 256
Z = 64
STEPS = 2
BANDS = 16


def block_levels(rng, extent, pieces, least, largest):
    gain = 1.0
    for axis_at, shards_of in pieces:
        heights = jax.random.uniform(jax.random.fold_in(jax.random.fold_in(rng, 6), axis_at), (shards_of,), jnp.float32, least / len(pieces), largest / len(pieces))
        gain = gain * jnp.repeat(jnp.exp(heights), extent[axis_at] // shards_of).reshape((-1,) + (1,) * (len(extent) - 1 - axis_at))
    return gain


def scatter_about(own_key, dims, scale, limit, split=(), held_as=jnp.bfloat16):
    gain = block_levels(own_key, dims, split, -0.22, 0.18) if split else 1.0
    result = jax.random.normal(own_key, dims, jnp.float32) * scale * gain
    return jnp.minimum(jnp.maximum(result, -limit), limit).astype(held_as)


def setup_inputs(seed: int = 0) -> dict:
    splits = jax.random.split(jax.random.key(seed), 7)
    phi_start = scatter_about(splits[0], (Z, BANDS, NX, NY), 1.0, 6.0, ((0, 8), (1, 4)), jnp.float32)
    coeff = jnp.clip(1.0 + 2.0 * jax.random.uniform(splits[1], (Z, NX, NY), jnp.float32) ** block_levels(splits[1], (Z, NX, NY), ((0, 8),), -0.2, 0.2), 1.0, 3.0)
    forward = scatter_about(splits[2], (STEPS, 2, Z, NX, NY), 1.0, 6.0, ((3, 8),), jnp.float32)
    rates = jnp.clip(jnp.exp(math.log(0.2) - 2.3025851 * jax.random.uniform(splits[3], (BANDS,), jnp.float32) ** block_levels(splits[3], (BANDS,), ((0, 4),), -0.2, 0.2)), 0.02, 0.2)
    speeds = jnp.clip(jnp.exp(math.log(2.0) - 1.3862944 * jax.random.uniform(splits[4], (BANDS,), jnp.float32) ** block_levels(splits[4], (BANDS,), ((0, 4),), -0.2, 0.2)), 0.5, 2.0)
    shares = jnp.clip(jnp.exp(math.log(0.12) - 1.7917595 * jax.random.uniform(splits[5], (BANDS,), jnp.float32) ** block_levels(splits[5], (BANDS,), ((0, 4),), -0.2, 0.2)), 0.02, 0.12)
    return dict(phi_start=phi_start, coeff=coeff, forward=forward, rates=rates, speeds=speeds, shares=shares)


def quadrature():
    level = jnp.arange(6).astype(jnp.float32)
    polar = 0.2 + 0.15 * level
    cosine = jnp.concatenate([-polar, polar])
    azimuth = jnp.concatenate([level * (math.pi / 3.0) + math.pi / 6.0, level * (math.pi / 3.0)])
    sine = jnp.sqrt(1.0 - cosine * cosine)
    return (cosine, sine * jnp.cos(azimuth), sine * jnp.sin(azimuth))

def frequency(count, start, length):
    index = jnp.arange(length, dtype=jnp.int32) + start
    signed = (index + count // 2) % count - count // 2
    return signed.astype(jnp.float32) * (1.5 * 2.0 * math.pi / count)

def sweep(source_re, source_im, inv_re, inv_im, couple, start_re, start_im, target_re, target_im, scale, reverse):
    depth = source_re.shape[0]
    blocks = depth // 8

    def fold(value):
        return value.reshape((blocks, 8) + value.shape[1:])
    cells = list(range(7, -1, -1)) if reverse else list(range(8))

    def block(carried, inputs):
        psi_real, psi_imag = carried
        rows_re, rows_im, aims_re, aims_im = inputs
        phi_real = [None] * 8
        phi_imag = [None] * 8
        sums = [None] * 8
        for cell in cells:
            sum_real = rows_re[cell] + couple * psi_real
            sum_imag = rows_im[cell] + couple * psi_imag
            psi_real = inv_re * sum_real - inv_im * sum_imag
            psi_imag = inv_re * sum_imag + inv_im * sum_real
            phi_real[cell] = lax.optimization_barrier(jnp.sum(psi_real, axis=0)) / 12.0
            phi_imag[cell] = lax.optimization_barrier(jnp.sum(psi_imag, axis=0)) / 12.0
            sums[cell] = lax.optimization_barrier(jnp.sum(psi_real * aims_re[cell] + psi_imag * aims_im[cell], axis=(2, 3))) * scale
        return ((psi_real, psi_imag), (jnp.stack(phi_real), jnp.stack(phi_imag), jnp.stack(sums)))
    carried, outputs = lax.scan(block, (start_re, start_im), (fold(source_re), fold(source_im), fold(target_re), fold(target_im)), reverse=reverse)

    def unfold(value):
        return value.reshape((depth,) + value.shape[2:])
    return (carried, unfold(outputs[0]), unfold(outputs[1]), unfold(outputs[2]))

def solve_modes(spec_re, spec_im, rates, speeds, shares, freq_x, freq_y, target_re, target_im, scale, wall_sum):
    cosine, along_x, along_y = quadrature()
    rate = rates[:, None, None]
    speed = speeds[:, None, None]
    source_re = spec_re * rate
    source_im = spec_im * rate
    wave = speed[None] * (along_x[:, None, None, None] * freq_x[:, None] + along_y[:, None, None, None] * freq_y[None, :])
    couple = jnp.abs(cosine)[:, None, None, None] * speed[None]
    real_part = rate[None] + couple
    denom = real_part * real_part + wave * wave
    inv_re = real_part / denom
    inv_im = -wave / denom
    zeros = jnp.zeros_like(inv_re[:6])
    down_end, down_re, down_im, down_grad = sweep(source_re, source_im, inv_re[:6], inv_im[:6], couple[:6], zeros, zeros, target_re, target_im, scale, True)
    weight = (jnp.abs(cosine[:6]) / 12.0)[:, None, None, None]
    flux_re = lax.optimization_barrier(jnp.sum(weight * down_end[0], axis=(0, 1)))
    flux_im = lax.optimization_barrier(jnp.sum(weight * down_end[1], axis=(0, 1)))
    flux_re, flux_im = wall_sum(flux_re, flux_im)
    share = shares[:, None, None]
    start_re = jnp.broadcast_to(share * flux_re, zeros.shape)
    start_im = jnp.broadcast_to(share * flux_im, zeros.shape)
    up_end, up_re, up_im, up_grad = sweep(source_re, source_im, inv_re[6:], inv_im[6:], couple[6:], start_re, start_im, target_re, target_im, scale, False)
    return (down_re + up_re, down_im + up_im, jnp.concatenate([down_grad, up_grad], axis=1))

def keep_flux(flux_re, flux_im):
    return (flux_re, flux_im)

def reference(phi_start, coeff, forward, rates, speeds, shares):
    phi = phi_start
    freq_x = frequency(NX, 0, NX)
    freq_y = frequency(NY, 0, NY)
    scale = 1.0 / NX
    grad = jnp.zeros((Z, 12, BANDS), jnp.float32)
    for step in range(STEPS):
        spec = jnp.fft.fft2(phi, axes=(2, 3), norm='ortho')
        new_re, new_im, grad_step = solve_modes(jnp.real(spec), jnp.imag(spec), rates, speeds, shares, freq_x, freq_y, forward[step, 0], forward[step, 1], scale, keep_flux)
        grad = grad + grad_step
        back = jnp.real(jnp.fft.ifft2(lax.complex(new_re, new_im), axes=(2, 3), norm='ortho'))
        phi = coeff[:, None] * back
    return (phi, grad)
```

```python
import functools
import math

import jax
import jax.numpy as jnp
import ml_dtypes
import numpy as np
from jax import lax
from jax.experimental import pallas as pl
from jax.experimental.pallas import tpu as pltpu
from jax.sharding import PartitionSpec as P

LANES = 128
VMEM = 56 * 1024 * 1024
CHUNK_ROWS = 16


def split_host(table):
    high = table.astype(ml_dtypes.bfloat16)
    low = (table - high.astype(np.float64)).astype(ml_dtypes.bfloat16)
    return high, low


def tables(count):
    half = count // 2
    index = np.arange(count)
    angle = (np.outer(index, index) % count) * (2.0 * np.pi / count)
    cos, sin = np.cos(angle) / math.sqrt(count), np.sin(angle) / math.sqrt(count)
    alternate = np.where(index % 2 == 0, 1.0, -1.0) / math.sqrt(count)
    into = np.concatenate([cos[:, :half], alternate[:, None], -sin[:, 1:half]], axis=1)
    weight = np.where(np.arange(half) == 0, 1.0, 2.0)[:, None]
    back = np.concatenate([weight * cos[:half], alternate[None], -2.0 * sin[1:half]], axis=0) / 12.0
    stacked = np.concatenate([cos, sin], axis=0)
    beside = np.concatenate([cos, sin], axis=1)
    return [part for table in (into, stacked, beside, back) for part in split_host(table)]


def quadrature():
    level = np.arange(6)
    polar = 0.2 + 0.15 * level
    cosine = np.concatenate([-polar, polar])
    azimuth = np.concatenate([level * (np.pi / 3.0) + np.pi / 6.0, level * (np.pi / 3.0)])
    sine = np.sqrt(1.0 - cosine * cosine)
    return (cosine, sine * np.cos(azimuth), sine * np.sin(azimuth))


def split(value):
    high = value.astype(jnp.bfloat16)
    low = (value - high.astype(jnp.float32)).astype(jnp.bfloat16)
    return high, low


def dot(left, right):
    return jnp.dot(left, right, preferred_element_type=jnp.float32)


def dot3(left, right):
    return dot(left[0], right[0]) + (dot(left[0], right[1]) + dot(left[1], right[0]))


class Plan:
    def __init__(self, shards, cells, bands, width, rows):
        self.shards, self.cells, self.bands, self.width, self.rows = shards, cells, bands, width, rows
        self.half = width // 2
        self.chunk = min(CHUNK_ROWS, rows)
        self.chunks = rows // self.chunk
        self.tiles = self.chunk // 2
        self.main = 2 * bands * self.chunk
        self.depth = shards * cells

    def height(self, chunk):
        return self.main + (16 if chunk == 0 else 0)

    def shape(self, chunk):
        return (self.shards, self.cells, self.height(chunk), LANES)


def forward_slabs(plan, phis, into, stacked, outs):
    width, half, rows, chunk = plan.width, plan.half, plan.rows, plan.chunk
    lane = lax.broadcasted_iota(jnp.int32, (width, half), 1)
    first = lane == 0
    columns = jnp.zeros((width, half), jnp.float32)
    for band in range(plan.bands):
        packed = dot3(split(phis(band)), into)
        both = dot3(stacked, split(packed))
        cos_re, cos_im = both[:width, :half], both[:width, half:]
        sin_re, sin_im = both[width:, :half], both[width:, half:]
        real = cos_re + jnp.where(first, 0.0, sin_im)
        imag = jnp.where(first, 0.0, cos_im) - sin_re
        for at in range(plan.chunks):
            for shard in range(plan.shards):
                start = shard * rows + at * chunk
                outs[at][shard, 0, band * chunk : (band + 1) * chunk, :] = real[start : start + chunk]
                low = (plan.bands + band) * chunk
                outs[at][shard, 0, low : low + chunk, :] = imag[start : start + chunk]
        place = 2 * band + 1
        columns = jnp.where(lane == place, pltpu.roll(cos_im, place, 1), columns)
        columns = jnp.where(lane == place + 8, -pltpu.roll(sin_im, place + 8, 1), columns)
    turned = columns.T[:16]
    slot = lax.broadcasted_iota(jnp.int32, (16, LANES), 1)
    for shard in range(plan.shards):
        start = shard * rows
        piece = turned[:, start // LANES * LANES : start // LANES * LANES + LANES]
        if start % LANES:
            piece = pltpu.roll(piece, LANES - start % LANES, 1)
        outs[0][shard, 0, plan.main :, :] = jnp.where(slot < rows, piece, 0.0)


def inverse_slabs(plan, ins, beside, back, take):
    width, half, rows, chunk = plan.width, plan.half, plan.rows, plan.chunk
    slot = lax.broadcasted_iota(jnp.int32, (16, LANES), 1)
    pieces = []
    for group in range(width // LANES):
        piece = jnp.zeros((16, LANES), jnp.float32)
        for shard in range(plan.shards):
            start = shard * rows
            if start // LANES == group:
                held = ins[0][shard, 0, plan.main :, :]
                if start % LANES:
                    held = pltpu.roll(held, start % LANES, 1)
                inside = (slot >= start % LANES) & (slot < start % LANES + rows)
                piece = jnp.where(inside, held, piece)
        pieces.append(piece)
    turned = jnp.concatenate(pieces, axis=1)
    columns = jnp.concatenate([turned, jnp.zeros((LANES - 16, width), jnp.float32)], axis=0).T
    first = lax.broadcasted_iota(jnp.int32, (width, half), 1) == 0
    for band in range(plan.bands):
        reals, imags = [], []
        for shard in range(plan.shards):
            for at in range(plan.chunks):
                reals.append(ins[at][shard, 0, band * chunk : (band + 1) * chunk, :])
                low = (plan.bands + band) * chunk
                imags.append(ins[at][shard, 0, low : low + chunk, :])
        real, imag = jnp.concatenate(reals, axis=0), jnp.concatenate(imags, axis=0)
        place = 2 * band + 1
        side_re = pltpu.roll(columns, LANES - place, 1)
        side_im = pltpu.roll(columns, LANES - place - 8, 1)
        upper = jnp.concatenate([real, jnp.where(first, side_re, imag)], axis=1)
        lower = jnp.concatenate([-imag, jnp.where(first, -side_im, real)], axis=1)
        mixed = dot3(beside, split(jnp.concatenate([upper, lower], axis=0)))
        take(band, dot3(split(mixed), back))


def first_kernel(plan, phi, into_h, into_l, stacked_h, stacked_l, *outs):
    forward_slabs(plan, lambda band: phi[0, band], (into_h[...], into_l[...]), (stacked_h[...], stacked_l[...]), outs)


def middle_kernel(plan, *refs):
    ins = refs[: plan.chunks]
    coeff = refs[plan.chunks]
    into_h, into_l, stacked_h, stacked_l, beside_h, beside_l, back_h, back_l = refs[plan.chunks + 1 : plan.chunks + 9]
    outs = refs[plan.chunks + 9 : 2 * plan.chunks + 9]
    held = refs[2 * plan.chunks + 9]

    def take(band, value):
        held[band] = value * coeff[0]

    inverse_slabs(plan, ins, (beside_h[...], beside_l[...]), (back_h[...], back_l[...]), take)
    forward_slabs(plan, lambda band: held[band], (into_h[...], into_l[...]), (stacked_h[...], stacked_l[...]), outs)


def last_kernel(plan, *refs):
    ins = refs[: plan.chunks]
    coeff, beside_h, beside_l, back_h, back_l, out = refs[plan.chunks :]

    def take(band, value):
        out[0, band] = value * coeff[0]

    inverse_slabs(plan, ins, (beside_h[...], beside_l[...]), (back_h[...], back_l[...]), take)


def whole(array):
    rank = len(array.shape)
    return pl.BlockSpec(array.shape, lambda cell: (0,) * rank)


def chunk_specs(plan):
    return [pl.BlockSpec((plan.shards, 1, plan.height(at), LANES), lambda cell: (0, cell, 0, 0)) for at in range(plan.chunks)]


def chunk_shapes(plan):
    return [jax.ShapeDtypeStruct(plan.shape(at), jnp.float32) for at in range(plan.chunks)]


def slab_spec(plan):
    return pl.BlockSpec((1, plan.bands, plan.width, plan.width), lambda cell: (cell, 0, 0, 0))


def coeff_spec(plan):
    return pl.BlockSpec((1, plan.width, plan.width), lambda cell: (cell, 0, 0))


def cost(plan, transforms):
    slabs = plan.cells * plan.bands
    return pl.CostEstimate(
        flops=transforms * slabs * 18 * plan.width**3, bytes_accessed=16 * slabs * plan.width**2, transcendentals=0
    )


def first(plan, phi, consts):
    return pl.pallas_call(
        functools.partial(first_kernel, plan),
        grid=(plan.cells,),
        in_specs=[slab_spec(plan)] + [whole(c) for c in consts[:4]],
        out_specs=chunk_specs(plan),
        out_shape=chunk_shapes(plan),
        compiler_params=pltpu.CompilerParams(vmem_limit_bytes=VMEM),
        cost_estimate=cost(plan, 1),
        name="into_modes",
    )(phi, *consts[:4])


def middle(plan, ins, coeff, consts):
    return pl.pallas_call(
        functools.partial(middle_kernel, plan),
        grid=(plan.cells,),
        in_specs=chunk_specs(plan) + [coeff_spec(plan)] + [whole(c) for c in consts],
        out_specs=chunk_specs(plan),
        out_shape=chunk_shapes(plan),
        scratch_shapes=[pltpu.VMEM((plan.bands, plan.width, plan.width), jnp.float32)],
        compiler_params=pltpu.CompilerParams(vmem_limit_bytes=VMEM),
        cost_estimate=cost(plan, 2),
        name="between_steps",
    )(*ins, coeff, *consts)


def last(plan, ins, coeff, consts):
    return pl.pallas_call(
        functools.partial(last_kernel, plan),
        grid=(plan.cells,),
        in_specs=chunk_specs(plan) + [coeff_spec(plan)] + [whole(c) for c in consts[4:]],
        out_specs=slab_spec(plan),
        out_shape=jax.ShapeDtypeStruct((plan.cells, plan.bands, plan.width, plan.width), jnp.float32),
        compiler_params=pltpu.CompilerParams(vmem_limit_bytes=VMEM),
        cost_estimate=cost(plan, 1),
        name="out_of_modes",
    )(*ins, coeff, *consts[4:])


def sweep_kernel(plan, at, upward, *refs):
    if upward:
        spec, aims, inv, couple, rate, part, start, keep, out, sums, totals = refs
    else:
        spec, aims, inv, couple, rate, out, flux, sums, totals = refs
    tiles, step_rows, depth = plan.tiles, plan.tiles, plan.depth
    imag_at = plan.bands * plan.chunk
    even = lax.broadcasted_iota(jnp.int32, (8, LANES), 0) % 2 == 0
    unroll = 4

    def rows(base, tile):
        return pl.ds(base + tile, 8, stride=step_rows)

    for tile in range(tiles + (1 if at == 0 else 0)):
        extra = tile == tiles
        inv_re = [inv[0, d, tile] for d in range(6)]
        inv_im = [inv[1, d, tile] for d in range(6)]

        def block(count, psi, tile=tile, extra=extra, inv_re=inv_re, inv_im=inv_im):
            psi_re, psi_im = list(psi[:6]), list(psi[6:])
            for inner in range(unroll):
                z = count * unroll + inner
                z = z if upward else depth - 1 - z
                if extra:
                    row_re = jnp.where(even, spec[z, rows(0, 0), :], spec[z, plan.main : plan.main + 8, :])
                    row_im = jnp.where(even, spec[z, rows(imag_at, 0), :], spec[z, plan.main + 8 : plan.main + 16, :])
                else:
                    row_re = spec[z, rows(0, tile), :]
                    row_im = spec[z, rows(imag_at, tile), :]
                row_re, row_im = rate[...] * row_re, rate[...] * row_im
                aim_re, aim_im = aims[z, 0, tile], aims[z, 1, tile]
                for d in range(6):
                    sum_re = row_re + couple[d] * psi_re[d]
                    sum_im = row_im + couple[d] * psi_im[d]
                    psi_re[d] = inv_re[d] * sum_re - inv_im[d] * sum_im
                    psi_im[d] = inv_re[d] * sum_im + inv_im[d] * sum_re
                    product = psi_re[d] * aim_re + psi_im[d] * aim_im
                    totals[d, z] = product if tile == 0 else totals[d, z] + product
                new_re = ((psi_re[0] + psi_re[1]) + (psi_re[2] + psi_re[3])) + (psi_re[4] + psi_re[5])
                new_im = ((psi_im[0] + psi_im[1]) + (psi_im[2] + psi_im[3])) + (psi_im[4] + psi_im[5])
                if extra:
                    at_re, at_im = slice(plan.main, plan.main + 8), slice(plan.main + 8, plan.main + 16)
                else:
                    at_re, at_im = rows(0, tile), rows(imag_at, tile)
                if upward:
                    new_re, new_im = new_re + part[z, at_re, :], new_im + part[z, at_im, :]
                if upward and extra:
                    pair = even & (keep[...] > 0.0)
                    main_re, main_im = out[z, rows(0, 0), :], out[z, rows(imag_at, 0), :]
                    out[z, rows(0, 0), :] = jnp.where(pair, 0.5 * (main_re + new_re), main_re)
                    out[z, rows(imag_at, 0), :] = jnp.where(pair, 0.5 * (main_im + new_im), main_im)
                out[z, at_re, :] = new_re
                out[z, at_im, :] = new_im
            return tuple(psi_re + psi_im)

        if upward:
            carried = (start[0, tile],) * 6 + (start[1, tile],) * 6
        else:
            carried = (jnp.zeros((8, LANES), jnp.float32),) * 12
        carried = lax.fori_loop(0, depth // unroll, block, carried)
        if not upward:
            cosine = [abs(float(c)) / 12.0 for c in quadrature()[0][:6]]
            for part_at in range(2):
                value = carried[6 * part_at] * cosine[0]
                for d in range(1, 6):
                    value = value + carried[6 * part_at + d] * cosine[d]
                value = value + pltpu.roll(value, 2, 0)
                flux[part_at, tile] = value + pltpu.roll(value, 4, 0)
    for d in range(6):
        sums[d] = jnp.sum(totals[d], axis=-1)


def sweep(plan, at, upward, *operands):
    tiles = plan.tiles + (1 if at == 0 else 0)
    out_shape = [jax.ShapeDtypeStruct((plan.depth, plan.height(at), LANES), jnp.float32)]
    if not upward:
        out_shape.append(jax.ShapeDtypeStruct((2, tiles, 8, LANES), jnp.float32))
    out_shape.append(jax.ShapeDtypeStruct((6, plan.depth, 8), jnp.float32))
    values = plan.depth * 6 * tiles * 8 * LANES
    return pl.pallas_call(
        functools.partial(sweep_kernel, plan, at, upward),
        in_specs=[pl.BlockSpec(memory_space=pltpu.VMEM)] * len(operands),
        out_specs=[pl.BlockSpec(memory_space=pltpu.VMEM)] * len(out_shape),
        out_shape=out_shape,
        scratch_shapes=[pltpu.VMEM((6, plan.depth, 8, LANES), jnp.float32)],
        compiler_params=pltpu.CompilerParams(vmem_limit_bytes=VMEM),
        cost_estimate=pl.CostEstimate(flops=values * 16, bytes_accessed=values * 4, transcendentals=0),
        name="upward" if upward else "downward",
    )(*operands)


def aims_kernel(plan, own, other, zeroth, lanes_turned, rows_turned, keep, edge, *outs):
    rows, half, chunk, tiles = plan.rows, plan.half, plan.chunk, plan.tiles
    cells = own.shape[1]
    held = outs[plan.chunks]
    row = lax.broadcasted_iota(jnp.int32, (cells * rows, half), 0) % rows
    lane = lax.broadcasted_iota(jnp.int32, (cells * rows, half), 1)
    owner = keep[...] > 0.0
    for part in range(2):
        sign = 1.0 if part == 0 else -1.0
        pairs = split(other[part].reshape(cells * rows, half))
        turned = dot(pairs[0], lanes_turned[...]) + dot(pairs[1], lanes_turned[...])
        pairs = split(turned)
        turned = dot(rows_turned[...], pairs[0]) + dot(rows_turned[...], pairs[1])
        pairs = split(zeroth[part])
        lead = dot(pairs[0], lanes_turned[...]) + dot(pairs[1], lanes_turned[...])
        lead = jnp.broadcast_to(lead[:, None, :], (cells, rows, half)).reshape(cells * rows, half)
        mirror = jnp.where(row == 0, jnp.where(owner[:1], 0.0, lead), turned)
        mirror = jnp.where(lane == 0, 0.0, mirror)
        held[...] = (own[part].reshape(cells * rows, half) + sign * mirror).reshape(cells, rows, half)
        partner = sign * jnp.where(owner[:1], lead, 0.0)
        partner = partner.reshape(cells, rows, half)
        for at in range(plan.chunks):
            for tile in range(tiles):
                for cell in range(cells):
                    pair = held[cell, pl.ds(at * chunk + tile, 2, stride=tiles), :]
                    outs[at][cell, part, tile] = jnp.concatenate([pair] * 4, axis=0)
        even = lax.broadcasted_iota(jnp.int32, (8, LANES), 0) % 2 == 0
        for cell in range(cells):
            side = jnp.broadcast_to(edge[part, cell : cell + 1], (8, LANES))
            outs[0][cell, part, tiles] = jnp.where(even, partner[cell, :8], side)


def make_aims(plan, own, other, zeroth, edge, keep, step):
    cells = 8
    rows, half = plan.rows, plan.half
    lanes_turned = np.zeros((half, half), ml_dtypes.bfloat16)
    rows_turned = np.zeros((cells * rows, cells * rows), ml_dtypes.bfloat16)
    for k in range(1, half):
        lanes_turned[half - k, k] = 1
    for c in range(cells):
        for r in range(1, rows):
            rows_turned[c * rows + r, c * rows + rows - r] = 1
    lanes_turned, rows_turned = jnp.asarray(lanes_turned), jnp.asarray(rows_turned)
    counts = [plan.tiles + (1 if at == 0 else 0) for at in range(plan.chunks)]
    return pl.pallas_call(
        functools.partial(aims_kernel, plan),
        grid=(plan.depth // cells,),
        in_specs=[
            pl.BlockSpec((None, 2, cells, rows, half), lambda z: (step, 0, z, 0, 0)),
            pl.BlockSpec((2, cells, rows, half), lambda z: (0, z, 0, 0)),
            pl.BlockSpec((2, cells, half), lambda z: (0, z, 0)),
            whole(lanes_turned),
            whole(rows_turned),
            whole(keep),
            pl.BlockSpec((2, cells, half), lambda z: (0, z, 0)),
        ],
        out_specs=[pl.BlockSpec((cells, 2, count, 8, LANES), lambda z: (z, 0, 0, 0, 0)) for count in counts],
        out_shape=[jax.ShapeDtypeStruct((plan.depth, 2, count, 8, LANES), jnp.float32) for count in counts],
        scratch_shapes=[pltpu.VMEM((cells, rows, half), jnp.float32)],
        compiler_params=pltpu.CompilerParams(vmem_limit_bytes=VMEM),
        name="targets",
    )(own, other, zeroth, lanes_turned, rows_turned, keep, edge)


def factors(plan, at, place, rate, speed):
    unit = 1.5 * 2.0 * math.pi / plan.width
    half, width = plan.half, plan.width
    base = place * plan.rows
    sub = jnp.arange(8) % 2
    row = base + at * plan.chunk + jnp.arange(plan.tiles)[:, None] + plan.tiles * sub[None, :]

    def signed(index):
        return ((index + half) % width - half).astype(jnp.float32) * unit

    freq_x = jnp.broadcast_to(signed(row)[:, :, None], (plan.tiles, 8, LANES))
    freq_y = jnp.broadcast_to(signed(jnp.arange(LANES)), (plan.tiles, 8, LANES))
    if at == 0:
        side_x = signed(base + jnp.arange(LANES))
        even = (sub == 0)[:, None]
        extra_x = jnp.where(even, -signed(base), side_x[None, :])
        extra_y = jnp.where(even, signed(jnp.arange(LANES))[None, :], signed(jnp.asarray(half)))
        freq_x = jnp.concatenate([freq_x, extra_x[None]], axis=0)
        freq_y = jnp.concatenate([freq_y, extra_y[None]], axis=0)
    cosine, along_x, along_y = [np.asarray(q, np.float32).reshape(12, 1, 1, 1) for q in quadrature()]
    wave = speed * (along_x * freq_x + along_y * freq_y)
    real = rate + np.abs(cosine) * speed
    denom = real * real + wave * wave
    return jnp.stack([real / denom, -wave / denom])


def body(phi_start, coeff, forward, rates, speeds, shares):
    shards = lax.axis_size("gx")
    groups = lax.axis_size("ba")
    place = lax.axis_index("gx")
    cells, bands, width, _ = phi_start.shape
    rows = forward.shape[3]
    plan = Plan(shards, cells, bands, width, rows)
    half, depth = plan.half, plan.depth
    consts = [jnp.asarray(part) for part in tables(width)]
    owner = place * rows == half
    keep = jnp.broadcast_to(jnp.where(owner, 1.0, 0.0).astype(jnp.float32), (8, LANES))

    def lift(value):
        return jnp.broadcast_to(jnp.repeat(value, 2)[:, None], (8, LANES))

    rate, speed, share = lift(rates), lift(speeds), lift(shares)
    polar = np.abs(np.asarray(quadrature()[0][:6], np.float32)).reshape(6, 1, 1)
    couple = polar * speed
    inverse = [factors(plan, at, place, rate, speed) for at in range(plan.chunks)]

    aims = []
    for step in range(forward.shape[0]):
        upper = forward[step, :, :, :, half:]
        other = lax.ppermute(upper, "gx", [(i, shards - 1 - i) for i in range(shards)])
        zeroth = lax.ppermute(upper[:, :, 0], "gx", [(i, (shards - i) % shards) for i in range(shards)])
        edge = jnp.pad(upper[..., 0], ((0, 0), (0, 0), (0, LANES - rows)))
        aims.append(make_aims(plan, forward, other, zeroth, edge, keep, step))

    def exchange(array):
        return lax.all_to_all(array, "gx", split_axis=0, concat_axis=0, tiled=True)

    down_sums, up_sums = [], []
    sent = first(plan, phi_start, consts)
    for step in range(forward.shape[0]):
        modes = [exchange(part).reshape((depth,) + part.shape[2:]) for part in sent]
        back = []
        for at in range(plan.chunks):
            spec = modes[at]
            inv = inverse[at]
            partial, flux, sums = sweep(plan, at, False, spec, aims[step][at], inv[:, :6], couple, rate)
            down_sums.append(sums)
            narrow = flux[:, :, :2]
            total = narrow
            for shift in range(1, groups):
                total = total + lax.ppermute(narrow, "ba", [(i, (i + shift) % groups) for i in range(groups)])
            start = share * jnp.concatenate([total] * 4, axis=2)
            new, sums = sweep(plan, at, True, spec, aims[step][at], inv[:, 6:], couple, rate, partial, start, keep)
            up_sums.append(sums)
            back.append(exchange(new.reshape(plan.shape(at))))
        if step + 1 < forward.shape[0]:
            sent = middle(plan, back, coeff, consts)
        else:
            phi = last(plan, back, coeff, consts)

    sums = jnp.stack([sum(down_sums), sum(up_sums)]).reshape(12, depth, bands, 2).sum(axis=3)
    sums = sums.transpose(1, 0, 2).reshape(shards, cells * 12 * bands) * (1.0 / width)
    grad = exchange(sums).sum(axis=0).reshape(cells, 12, bands)
    return (phi, grad)


def solution(mesh):
    in_specs = (
        P("gx", "ba", None, None),
        P("gx", None, None),
        P(None, None, None, "gx", None),
        P("ba"),
        P("ba"),
        P("ba"),
    )
    out_specs = (P("gx", "ba", None, None), P("gx", None, "ba"))
    return jax.shard_map(body, mesh=mesh, in_specs=in_specs, out_specs=out_specs, check_vma=False)
```

```python
import functools
import math

import jax
import jax.numpy as jnp
import ml_dtypes
import numpy as np
from jax import lax
from jax.experimental import pallas as pl
from jax.experimental.pallas import tpu as pltpu
from jax.sharding import PartitionSpec as P

LANES = 128
VMEM = 56 * 1024 * 1024
CHUNK_ROWS = 16


def split_host(table):
    high = table.astype(ml_dtypes.bfloat16)
    low = (table - high.astype(np.float64)).astype(ml_dtypes.bfloat16)
    return high, low


def tables(count):
    half = count // 2
    index = np.arange(count)
    angle = (np.outer(index, index) % count) * (2.0 * np.pi / count)
    cos, sin = np.cos(angle) / math.sqrt(count), np.sin(angle) / math.sqrt(count)
    alternate = np.where(index % 2 == 0, 1.0, -1.0) / math.sqrt(count)
    into = np.concatenate([cos[:, :half], alternate[:, None], -sin[:, 1:half]], axis=1)
    weight = np.where(np.arange(half) == 0, 1.0, 2.0)[:, None]
    back = np.concatenate([weight * cos[:half], alternate[None], -2.0 * sin[1:half]], axis=0) / 12.0
    stacked = np.concatenate([cos, sin], axis=0)
    beside = np.concatenate([cos, sin], axis=1)
    return [part for table in (into, stacked, beside, back) for part in split_host(table)]


def quadrature():
    level = np.arange(6)
    polar = 0.2 + 0.15 * level
    cosine = np.concatenate([-polar, polar])
    azimuth = np.concatenate([level * (np.pi / 3.0) + np.pi / 6.0, level * (np.pi / 3.0)])
    sine = np.sqrt(1.0 - cosine * cosine)
    return (cosine, sine * np.cos(azimuth), sine * np.sin(azimuth))


def split(value):
    high = value.astype(jnp.bfloat16)
    low = (value - high.astype(jnp.float32)).astype(jnp.bfloat16)
    return high, low


def dot(left, right):
    return jnp.dot(left, right, preferred_element_type=jnp.float32)


def dot3(left, right):
    return dot(left[0], right[0]) + (dot(left[0], right[1]) + dot(left[1], right[0]))


class Plan:
    def __init__(self, shards, cells, width, rows):
        self.shards, self.cells, self.width, self.rows = shards, cells, width, rows
        self.half = width // 2
        self.chunk = min(CHUNK_ROWS, rows)
        self.chunks = rows // self.chunk
        self.tiles = self.chunk // 4
        self.main = 4 * self.chunk
        self.depth = shards * cells
        self.edge = cells * self.main
        self.pad = (cells + 7) // 8 * 8

    def height(self, chunk):
        return self.edge + (self.pad if chunk == 0 else 0)

    def shapes(self, chunk, sides):
        return [jax.ShapeDtypeStruct((self.shards, 2 // sides * self.height(chunk), LANES), jnp.float32)] * sides

    def sides_sent(self, chunk):
        return 2 if chunk == 0 else 1

    def sides_back(self, chunk):
        return 2 if chunk == self.chunks - 1 else 1

    def steps(self, chunk):
        return self.tiles + (1 if chunk == 0 else 0)


class View:
    def __init__(self, ref, offset=0):
        self.ref, self.offset = ref, offset

    def moved(self, rows):
        return pl.ds(self.offset + rows.start, rows.size, stride=rows.stride)

    def at(self, shard, rows):
        return self.ref[shard, self.moved(rows), :]

    def put(self, shard, rows, value):
        self.ref[shard, self.moved(rows), :] = value


def views(plan, at, refs):
    if len(refs) == 2:
        return [View(ref) for ref in refs]
    return [View(refs[0], side * plan.height(at)) for side in range(2)]


def forward_slabs(plan, cell, phis, into, stacked, outs):
    width, half, rows, chunk = plan.width, plan.half, plan.rows, plan.chunk
    lane = lax.broadcasted_iota(jnp.int32, (width, half), 1)
    first = lane == 0
    columns = jnp.zeros((width, half), jnp.float32)
    for band in range(2):
        packed = dot3(split(phis(band)), into)
        both = dot3(stacked, split(packed))
        cos_re, cos_im = both[:width, :half], both[:width, half:]
        sin_re, sin_im = both[width:, :half], both[width:, half:]
        real = cos_re + jnp.where(first, 0.0, sin_im)
        imag = jnp.where(first, 0.0, cos_im) - sin_re
        for at in range(plan.chunks):
            base = pl.multiple_of(cell * plan.main, 8) if at == 0 else 0
            for shard in range(plan.shards):
                start = shard * rows + at * chunk
                outs[at][shard, pl.ds(base + band * chunk, chunk), :] = real[start : start + chunk]
                outs[at][shard, pl.ds(base + (2 + band) * chunk, chunk), :] = imag[start : start + chunk]
        columns = jnp.where(lane == band, pltpu.roll(cos_im, band, 1) if band else cos_im, columns)
        columns = jnp.where(lane == band + 2, -pltpu.roll(sin_im, band + 2, 1), columns)
    turned = columns.T[:8]
    slot = lax.broadcasted_iota(jnp.int32, (1, LANES), 1)
    for shard in range(plan.shards):
        start = shard * rows
        piece = turned[:, start // LANES * LANES : start // LANES * LANES + LANES]
        row = jnp.zeros((1, LANES), jnp.float32)
        for group in range(4):
            shift = (group * rows - start) % LANES
            held = pltpu.roll(piece, shift, 1) if shift else piece
            row = jnp.where((slot >= group * rows) & (slot < (group + 1) * rows), held[group : group + 1], row)
        outs[0][shard, pl.ds(plan.edge + cell, 1), :] = row


def inverse_slabs(plan, cell, ins, beside, back, take):
    width, half, rows, chunk = plan.width, plan.half, plan.rows, plan.chunk
    lines = [ins[0][shard, pl.ds(plan.edge + cell, 1), :] for shard in range(plan.shards)]
    lines.append(jnp.zeros((LANES - plan.shards, LANES), jnp.float32))
    turned = jnp.concatenate(lines, axis=0).T[: 4 * rows]
    shifted = [pltpu.roll(turned, LANES - shard, 1) if shard else turned for shard in range(plan.shards)]
    sides = [jnp.concatenate([held[g * rows : (g + 1) * rows] for held in shifted], axis=0) for g in range(4)]
    first = lax.broadcasted_iota(jnp.int32, (width, half), 1) == 0
    for band in range(2):
        reals, imags = [], []
        for shard in range(plan.shards):
            for at in range(plan.chunks):
                base = pl.multiple_of(cell * plan.main, 8) if at == 0 else 0
                reals.append(ins[at][shard, pl.ds(base + band * chunk, chunk), :])
                imags.append(ins[at][shard, pl.ds(base + (2 + band) * chunk, chunk), :])
        real, imag = jnp.concatenate(reals, axis=0), jnp.concatenate(imags, axis=0)
        upper = jnp.concatenate([real, jnp.where(first, sides[band], imag)], axis=1)
        lower = jnp.concatenate([-imag, jnp.where(first, -sides[band + 2], real)], axis=1)
        mixed = dot3(beside, split(jnp.concatenate([upper, lower], axis=0)))
        take(band, dot3(split(mixed), back))


def first_kernel(plan, kept, phi, into_h, into_l, stacked_h, stacked_l, *refs):
    cell = pl.program_id(0)
    outs = refs[kept:]
    into, stacked = (into_h[...], into_l[...]), (stacked_h[...], stacked_l[...])
    forward_slabs(plan, cell, lambda band: phi[0, band], into, stacked, outs)


def middle_kernel(plan, kept, *refs):
    cell = pl.program_id(0)
    ins = refs[: plan.chunks]
    coeff = refs[plan.chunks]
    into_h, into_l, stacked_h, stacked_l, beside_h, beside_l, back_h, back_l = refs[plan.chunks + 1 : plan.chunks + 9]
    outs, held = refs[plan.chunks + 9 + kept : -1], refs[-1]

    def take(band, value):
        held[band] = value * coeff[0]

    inverse_slabs(plan, cell, ins, (beside_h[...], beside_l[...]), (back_h[...], back_l[...]), take)
    into, stacked = (into_h[...], into_l[...]), (stacked_h[...], stacked_l[...])
    forward_slabs(plan, cell, lambda band: held[band], into, stacked, outs)


def last_kernel(plan, *refs):
    ins = refs[: plan.chunks]
    coeff, beside_h, beside_l, back_h, back_l = refs[plan.chunks : plan.chunks + 5]
    out = refs[-1]

    def take(band, value):
        out[0, band] = value * coeff[0]

    inverse_slabs(plan, pl.program_id(0), ins, (beside_h[...], beside_l[...]), (back_h[...], back_l[...]), take)


def whole(array):
    rank = len(array.shape)
    return pl.BlockSpec(array.shape, lambda cell: (0,) * rank)


def piece_specs(plan, side, sides):
    specs = []
    for at in range(plan.chunks):
        merged = sides(at) == 1
        if at == 0:
            shape = (plan.shards, plan.height(0), LANES)
            specs.append(pl.BlockSpec(shape, lambda cell, first=side if merged else 0: (0, first, 0)))
        else:
            shape = (plan.shards, plan.main, LANES)
            specs.append(pl.BlockSpec(shape, lambda cell, first=side * plan.cells if merged else 0: (0, first + cell, 0)))
    return specs


def sent_shapes(plan):
    return [plan.shapes(at, plan.sides_sent(at))[0] for at in range(plan.chunks)]


def slab_spec(plan, side):
    return pl.BlockSpec((1, 2, plan.width, plan.width), lambda cell: (cell, side, 0, 0))


def coeff_spec(plan):
    return pl.BlockSpec((1, plan.width, plan.width), lambda cell: (cell, 0, 0))


def cost(microseconds):
    return pl.CostEstimate(flops=0, bytes_accessed=int(microseconds * 3.69e6), transcendentals=0)


PARAMS = pltpu.CompilerParams(vmem_limit_bytes=VMEM)


def send(kernel, plan, side, operands, in_specs, held, microseconds, scratch, name):
    aliases = {}
    for at in range(plan.chunks):
        if held is not None and plan.sides_sent(at) == 1:
            aliases[len(operands)] = at
            operands, in_specs = operands + [held[at]], in_specs + [pl.BlockSpec(memory_space=pl.ANY)]
    return pl.pallas_call(
        functools.partial(kernel, plan, len(aliases)),
        grid=(plan.cells,),
        in_specs=in_specs,
        out_specs=piece_specs(plan, side, plan.sides_sent),
        out_shape=sent_shapes(plan),
        input_output_aliases=aliases,
        scratch_shapes=scratch,
        compiler_params=PARAMS,
        cost_estimate=cost(microseconds),
        name=name,
    )(*operands)


def first(plan, side, phi, consts, held):
    in_specs = [slab_spec(plan, side)] + [whole(c) for c in consts[:4]]
    return send(first_kernel, plan, side, [phi, *consts[:4]], in_specs, held, 12, [], "into_modes")


def middle(plan, side, ins, coeff, consts, held):
    in_specs = piece_specs(plan, side, plan.sides_back) + [coeff_spec(plan)] + [whole(c) for c in consts]
    scratch = [pltpu.VMEM((2, plan.width, plan.width), jnp.float32)]
    return send(middle_kernel, plan, side, [*ins, coeff, *consts], in_specs, held, 25, scratch, "between_steps")


def last(plan, side, ins, coeff, consts, held):
    operands = [*ins, coeff, *consts[4:]]
    in_specs = piece_specs(plan, side, plan.sides_back) + [coeff_spec(plan)] + [whole(c) for c in consts[4:]]
    aliases = {}
    if held is not None:
        aliases = {len(operands): 0}
        operands.append(held)
        in_specs.append(pl.BlockSpec(memory_space=pl.ANY))
    return pl.pallas_call(
        functools.partial(last_kernel, plan),
        grid=(plan.cells,),
        in_specs=in_specs,
        out_specs=slab_spec(plan, side),
        out_shape=jax.ShapeDtypeStruct((plan.cells, 4, plan.width, plan.width), jnp.float32),
        input_output_aliases=aliases,
        compiler_params=PARAMS,
        cost_estimate=cost(16),
        name="out_of_modes",
    )(*operands)


def sweep_kernel(plan, at, upward, groups, *refs):
    refs = list(refs)

    def pop(count):
        taken = refs[:count]
        del refs[:count]
        return taken

    specs = views(plan, at, pop(plan.sides_sent(at)))
    aims, inv, couple, rate = pop(4)
    if upward:
        parts = views(plan, at, pop(2))
        extras = pop(1)[0] if at == 0 else None
        share, keep = pop(2)
        fluxes = pop(groups)
        outs = views(plan, at, pop(plan.sides_back(at)))
        sums, totals = refs
    else:
        outs = views(plan, at, pop(2))
        flux, sums = pop(2)
        extras = pop(1)[0] if at == 0 else None
        totals = refs[0]
    tiles, depth, cells, main, rows = plan.tiles, plan.depth, plan.cells, plan.main, plan.rows
    imag_at = 2 * plan.chunk
    sub = lax.broadcasted_iota(jnp.int32, (8, LANES), 0)
    lane = lax.broadcasted_iota(jnp.int32, (1, LANES), 1)
    zeros = jnp.zeros((8, LANES), jnp.float32)
    cosine = [abs(float(c)) / 12.0 for c in quadrature()[0][:6]]

    def place(cell, base, tile):
        return pl.ds(cell * main + base + tile, 8, stride=tiles)

    def extra_source(shard, cell, base):
        edge = []
        for s in range(2):
            line = specs[s].at(shard, pl.ds(plan.edge + cell, 1))
            line = pltpu.roll(line, LANES - 2 * rows, 1) if base else line
            edge.append(jnp.where(sub < 4, line, pltpu.roll(line, LANES - rows, 1)))
        row0 = [specs[s].at(shard, place(cell, base, 0)) for s in range(2)]
        kind = sub % 4
        value = jnp.where(kind == 0, row0[0], jnp.where(kind == 1, pltpu.roll(row0[1], 1, 0), 0.0))
        return jnp.where(kind == 2, edge[0], jnp.where(kind == 3, edge[1], value))

    def extra_store(shard, cell, new_re, new_im):
        if not upward:
            extras[shard * cells + cell, 0] = new_re
            extras[shard * cells + cell, 1] = new_im
            return
        new_re = new_re + extras[shard * cells + cell, 0]
        new_im = new_im + extras[shard * cells + cell, 1]
        spread = [new_re, pltpu.roll(new_re, rows, 1), pltpu.roll(new_im, 2 * rows, 1), pltpu.roll(new_im, 3 * rows, 1)]
        for side in range(2):
            row = spread[0][2 + side : 3 + side]
            for group in range(1, 4):
                at_sub = 2 + side + 4 * (group % 2)
                row = jnp.where(lane < group * rows, row, spread[group][at_sub : at_sub + 1])
            outs[side].put(shard, pl.ds(plan.edge + cell, 1), row)
            for base, value in ((0, new_re), (imag_at, new_im)):
                value = pltpu.roll(value, 7, 0) if side else value
                held = outs[side].at(shard, place(cell, base, 0))
                pair = (sub % 4 == 0) & (keep[...] > 0.0)
                outs[side].put(shard, place(cell, base, 0), jnp.where(pair, 0.5 * (held + value), held))

    for count in range(2 * tiles + (1 if at == 0 else 0)):
        extra = count == 2 * tiles
        side, tile = (2, tiles) if extra else (count // tiles, count % tiles)
        inv_re = [inv[0, d, count] for d in range(6)]
        inv_im = [inv[1, d, count] for d in range(6)]
        fresh = extra or tile == 0

        def block(step, psi, extra=extra, side=side, tile=tile, inv_re=inv_re, inv_im=inv_im, fresh=fresh):
            psi_re, psi_im = list(psi[:6]), list(psi[6:])
            shard = step if upward else plan.shards - 1 - step
            for cell in range(cells) if upward else range(cells - 1, -1, -1):
                z = shard * cells + cell
                if extra:
                    row_re, row_im = extra_source(shard, cell, 0), extra_source(shard, cell, imag_at)
                else:
                    row_re = specs[side].at(shard, place(cell, 0, tile))
                    row_im = specs[side].at(shard, place(cell, imag_at, tile))
                row_re, row_im = rate[side] * row_re, rate[side] * row_im
                aim_re, aim_im = aims[z, 0, tile], aims[z, 1, tile]
                for d in range(6):
                    sum_re = row_re + couple[side, d] * psi_re[d]
                    sum_im = row_im + couple[side, d] * psi_im[d]
                    psi_re[d] = inv_re[d] * sum_re - inv_im[d] * sum_im
                    psi_im[d] = inv_re[d] * sum_im + inv_im[d] * sum_re
                    product = psi_re[d] * aim_re + psi_im[d] * aim_im
                    totals[side, d, z] = product if fresh else totals[side, d, z] + product
                new_re = ((psi_re[0] + psi_re[1]) + (psi_re[2] + psi_re[3])) + (psi_re[4] + psi_re[5])
                new_im = ((psi_im[0] + psi_im[1]) + (psi_im[2] + psi_im[3])) + (psi_im[4] + psi_im[5])
                if extra:
                    extra_store(shard, cell, new_re, new_im)
                    continue
                if upward:
                    new_re = new_re + parts[side].at(shard, place(cell, 0, tile))
                    new_im = new_im + parts[side].at(shard, place(cell, imag_at, tile))
                outs[side].put(shard, place(cell, 0, tile), new_re)
                outs[side].put(shard, place(cell, imag_at, tile), new_im)
            return tuple(psi_re + psi_im)

        if upward:
            start = []
            for part in range(2):
                value = fluxes[0][part, tile]
                for other in fluxes[1:]:
                    value = value + other[part, tile]
                start += [share[side] * value] * 6
        else:
            start = [zeros] * 12
        carried = lax.fori_loop(0, plan.shards, block, tuple(start))
        if not upward:
            for part in range(2):
                value = carried[6 * part] * cosine[0]
                for d in range(1, 6):
                    value = value + carried[6 * part + d] * cosine[d]
                value = value + pltpu.roll(value, 4, 0)
                if extra:
                    swapped = jnp.where(sub % 2 == 0, pltpu.roll(value, 7, 0), pltpu.roll(value, 1, 0))
                    flux[part, tile] = value + swapped
                elif side == 0:
                    flux[part, tile] = value
                else:
                    flux[part, tile] = flux[part, tile] + value
    for side in range(3 if at == 0 else 2):
        for d in range(6):
            sums[side, d] = jnp.sum(totals[side, d], axis=-1)


def sweep(plan, at, upward, groups, *operands):
    tiles = plan.steps(at)
    sides = 3 if at == 0 else 2
    vmem = pl.BlockSpec(memory_space=pltpu.VMEM)
    out_shape = plan.shapes(at, plan.sides_back(at) if upward else 2)
    if not upward:
        out_shape.append(jax.ShapeDtypeStruct((2, tiles, 8, LANES), jnp.float32))
    out_shape.append(jax.ShapeDtypeStruct((sides, 6, plan.depth, 8), jnp.float32))
    if not upward and at == 0:
        out_shape.append(jax.ShapeDtypeStruct((plan.depth, 2, 8, LANES), jnp.float32))
    return pl.pallas_call(
        functools.partial(sweep_kernel, plan, at, upward, groups),
        in_specs=[vmem] * len(operands),
        out_specs=[vmem] * len(out_shape),
        out_shape=out_shape,
        scratch_shapes=[pltpu.VMEM((sides, 6, plan.depth, 8, LANES), jnp.float32)],
        compiler_params=PARAMS,
        cost_estimate=cost(13),
        name="upward" if upward else "downward",
    )(*operands)


def mirror_kernel(plan, group, upper, lanes_turned, rows_turned, turned, lead):
    rows, half = plan.rows, plan.half
    cells = upper.shape[1]
    for part in range(2):
        sign = 1.0 if part == 0 else -1.0
        pairs = split(sign * upper[part].reshape(cells * rows, half))
        value = dot(pairs[0], lanes_turned[...]) + dot(pairs[1], lanes_turned[...])
        lead[part] = value.reshape(cells, rows, half)[:, 0, :]
        pairs = split(value)
        value = dot(rows_turned[...], pairs[0]) + dot(rows_turned[...], pairs[1])
        turned[part] = value.reshape(cells, rows, half)


def mirror(plan, forward, groups):
    cells = 8
    rows, half = plan.rows, plan.half
    share = plan.depth // groups
    lanes_turned = np.zeros((half, half), ml_dtypes.bfloat16)
    rows_turned = np.zeros((cells * rows, cells * rows), ml_dtypes.bfloat16)
    for k in range(1, half):
        lanes_turned[half - k, k] = 1
    for c in range(cells):
        for r in range(1, rows):
            rows_turned[c * rows + r, c * rows + rows - r] = 1
    lanes_turned, rows_turned = jnp.asarray(lanes_turned), jnp.asarray(rows_turned)
    blocks = share // cells
    group = lax.axis_index("ba").astype(jnp.int32).reshape(1)
    spec = pltpu.PrefetchScalarGridSpec(
        num_scalar_prefetch=1,
        grid=(forward.shape[0], blocks),
        in_specs=[
            pl.BlockSpec((None, 2, cells, rows, half), lambda step, z, at: (step, 0, at[0] * blocks + z, 0, 1)),
            pl.BlockSpec(lanes_turned.shape, lambda step, z, at: (0, 0)),
            pl.BlockSpec(rows_turned.shape, lambda step, z, at: (0, 0)),
        ],
        out_specs=[
            pl.BlockSpec((None, 2, cells, rows, half), lambda step, z, at: (step, 0, z, 0, 0)),
            pl.BlockSpec((None, 2, cells, half), lambda step, z, at: (step, 0, z, 0)),
        ],
    )
    return pl.pallas_call(
        functools.partial(mirror_kernel, plan),
        grid_spec=spec,
        out_shape=[
            jax.ShapeDtypeStruct((forward.shape[0], 2, share, rows, half), jnp.float32),
            jax.ShapeDtypeStruct((forward.shape[0], 2, share, half), jnp.float32),
        ],
        compiler_params=PARAMS,
        cost_estimate=cost(5),
        name="mirrored",
    )(group, forward, lanes_turned, rows_turned)


def aims_kernel(plan, group, own, other, keep, *refs):
    outs, held = refs[:-1], refs[-1]
    rows, half, chunk, tiles = plan.rows, plan.half, plan.chunk, plan.tiles
    cells = own.shape[1]
    owner = keep[...] > 0.0
    row = lax.broadcasted_iota(jnp.int32, (rows, half), 0)
    sub = lax.broadcasted_iota(jnp.int32, (8, LANES), 0)
    lane = lax.broadcasted_iota(jnp.int32, (1, LANES), 1)
    for part in range(2):
        line = own[part, :, :, half:].reshape(cells * rows, half).T[:1]
        if cells * rows < LANES:
            line = jnp.concatenate([line, jnp.zeros((1, LANES - cells * rows), jnp.float32)], axis=1)
        for cell in range(cells):
            mine, theirs = own[part, cell, :, :half], other[part, cell]
            held[...] = mine + jnp.where((row == 0) & owner[:1], 0.0, theirs)
            for at in range(plan.chunks):
                for tile in range(tiles):
                    four = held[pl.ds(at * chunk + tile, 4, stride=tiles), :]
                    outs[at][cell, part, tile] = jnp.concatenate([four, four], axis=0)
            partner = jnp.where(owner, theirs[:1], 0.0)
            start = cell * rows
            piece = line[:, start // LANES * LANES : start // LANES * LANES + LANES]
            at_zero = pltpu.roll(piece, LANES - start % LANES, 1) if start % LANES else piece
            outs[0][cell, part, tiles] = jnp.where(sub % 4 < 2, partner, jnp.where(lane < rows, at_zero, 0.0))


def make_aims(plan, own, other, keep, step):
    cells = 8
    rows, half = plan.rows, plan.half
    groups = other.shape[0]
    blocks = other.shape[2] // cells
    group = lax.axis_index("ba").astype(jnp.int32).reshape(1)

    def sender(z, at):
        return (lax.rem(at[0] + groups - z // blocks, groups), 0, z % blocks, 0, 0)

    spec = pltpu.PrefetchScalarGridSpec(
        num_scalar_prefetch=1,
        grid=(plan.depth // cells,),
        in_specs=[
            pl.BlockSpec((None, 2, cells, rows, plan.width), lambda z, at: (step, 0, z, 0, 0)),
            pl.BlockSpec((None, 2, cells, rows, half), sender),
            pl.BlockSpec(keep.shape, lambda z, at: (0, 0)),
        ],
        out_specs=[pl.BlockSpec((cells, 2, plan.steps(at), 8, LANES), lambda z, at: (z, 0, 0, 0, 0)) for at in range(plan.chunks)],
        scratch_shapes=[pltpu.VMEM((rows, half), jnp.float32)],
    )
    return pl.pallas_call(
        functools.partial(aims_kernel, plan),
        grid_spec=spec,
        out_shape=[jax.ShapeDtypeStruct((plan.depth, 2, plan.steps(at), 8, LANES), jnp.float32) for at in range(plan.chunks)],
        compiler_params=PARAMS,
        cost_estimate=cost(8),
        name="targets",
    )(group, own, other, keep)


def lift(value):
    main = jnp.broadcast_to(value.reshape(2, 2, 1), (2, 2, 4)).reshape(2, 8)
    extra = jnp.broadcast_to(value.reshape(2, 2).T[:, None, :], (2, 2, 2)).reshape(1, 8)
    return jnp.broadcast_to(jnp.concatenate([main, extra])[:, :, None], (3, 8, LANES))


def factors(plan, at, place, rate, speed):
    unit = 1.5 * 2.0 * math.pi / plan.width
    half, width, tiles = plan.half, plan.width, plan.tiles
    base = place * plan.rows
    sub = jnp.arange(8)

    def signed(index):
        return ((index + half) % width - half).astype(jnp.float32) * unit

    row = base + at * plan.chunk + jnp.arange(tiles)[:, None] + tiles * (sub % 4)[None, :]
    freq_x = jnp.broadcast_to(signed(row)[None, :, :, None], (2, tiles, 8, LANES)).reshape(2 * tiles, 8, LANES)
    freq_y = jnp.broadcast_to(signed(jnp.arange(LANES)), (2 * tiles, 8, LANES))
    sides = [0] * tiles + [1] * tiles
    if at == 0:
        partner = (sub % 4 < 2)[:, None]
        extra_x = jnp.where(partner, -signed(base), signed(base + jnp.arange(LANES) % plan.rows)[None, :])
        extra_y = jnp.where(partner, signed(jnp.arange(LANES))[None, :], signed(jnp.asarray(half)))
        freq_x = jnp.concatenate([freq_x, extra_x[None]], axis=0)
        freq_y = jnp.concatenate([freq_y, extra_y[None]], axis=0)
        sides.append(2)
    rate, speed = [jnp.concatenate([v[s : s + 1] for s in sides]) for v in (rate, speed)]
    cosine, along_x, along_y = [np.asarray(q, np.float32).reshape(12, 1, 1, 1) for q in quadrature()]
    wave = speed * (along_x * freq_x + along_y * freq_y)
    real = rate + np.abs(cosine) * speed
    denom = real * real + wave * wave
    return jnp.stack([real / denom, -wave / denom])


def body(phi_start, coeff, forward, rates, speeds, shares):
    shards = lax.axis_size("gx")
    groups = lax.axis_size("ba")
    place = lax.axis_index("gx")
    cells, bands, width, _ = phi_start.shape
    rows = forward.shape[3]
    steps = forward.shape[0]
    plan = Plan(shards, cells, width, rows)
    depth = plan.depth
    consts = [jnp.asarray(part) for part in tables(width)]
    owner = place * rows == plan.half
    keep = jnp.broadcast_to(jnp.where(owner, 1.0, 0.0).astype(jnp.float32), (8, LANES))
    rate, speed, share = lift(rates), lift(speeds), lift(shares)
    polar = np.abs(np.asarray(quadrature()[0][:6], np.float32)).reshape(1, 6, 1, 1)
    couple = polar * speed[:, None]
    inverse = [factors(plan, at, place, rate, speed) for at in range(plan.chunks)]

    def tie(value, *others):
        return lax.optimization_barrier((value, *others))[0]

    def swap_targets(turned, lead):
        turned = lax.ppermute(turned, "gx", [(i, shards - 1 - i) for i in range(shards)])
        lead = lax.ppermute(lead, "gx", [(i, (shards - i) % shards) for i in range(shards)])
        return jnp.where(jnp.arange(rows)[:, None] == 0, lead[:, :, :, None, :], turned)

    def spread_targets(turned):
        parts = [turned]
        for shift in range(1, groups):
            parts.append(lax.ppermute(turned, "ba", [(i, (i + shift) % groups) for i in range(groups)]))
        return parts

    def exchange(array):
        return lax.all_to_all(array, "gx", split_axis=0, concat_axis=0, tiled=True)

    main_sums, extra_sums = [[], []], [[], []]

    def collect(sums, way):
        main_sums[way].append(sums[:2])
        if sums.shape[0] == 3:
            extra_sums[way].append(sums[2])

    def into(transform):
        pieces, held = [[] for _ in range(plan.chunks)], None
        for side in range(2):
            held = transform(side, held)
            for at in range(plan.chunks):
                if plan.sides_sent(at) == 2 or side == 1:
                    pieces[at].append(held[at])
        return pieces

    def in_order(pieces, after, besides=()):
        arrived = []
        for piece in pieces:
            if after is not None:
                piece = tie(piece, after, *besides)
            after = exchange(piece)
            arrived.append(after)
        return arrived

    flipped = mirror(plan, forward, groups)
    swapped = swap_targets(*flipped)
    starts = [tie(phi_start, *flipped), tie(phi_start, swapped)]
    sent = into(lambda side, held: first(plan, side, starts[side], consts, held))
    spread = [spread_targets(swapped[step]) for step in range(steps)]
    aims = [None] * steps
    for step in range(steps):
        modes, after = [], None
        for at in range(plan.chunks):
            besides = spread[0][1 : 2 if at == 0 and plan.chunks > 1 else groups] if step == 0 else ()
            modes.append(in_order(sent[at], after, besides))
            after = modes[at][-1]
        if step == 0:
            aims[0] = make_aims(plan, forward, jnp.stack(spread[0]), keep, 0)
        back = []
        for at in range(plan.chunks):
            inv = inverse[at]
            common = (*modes[at], aims[step][at])
            part0, part1, flux, sums, *extras = sweep(plan, at, False, groups, *common, inv[:, :6], couple, rate)
            collect(sums, 0)
            fluxes = [flux]
            for shift in range(1, groups):
                fluxes.append(lax.ppermute(flux, "ba", [(i, (i + shift) % groups) for i in range(groups)]))
            rest = (part0, part1, *extras, share, keep, *fluxes)
            *new, sums = sweep(plan, at, True, groups, *common, inv[:, 6:], couple, rate, *rest)
            collect(sums, 1)
            if step + 1 < steps and at == 0:
                new[0] = tie(new[0], *spread[step + 1])
            if step + 1 < steps and at == plan.chunks - 1:
                aims[step + 1] = make_aims(plan, forward, jnp.stack(spread[step + 1]), keep, step + 1)
                new[0] = tie(new[0], *aims[step + 1])
            back.append(in_order(new, back[-1][-1] if back else None))
        ends = [[pieces[side % len(pieces)] for pieces in back] for side in range(2)]
        if step + 1 < steps:
            sent = into(lambda side, held: middle(plan, side, ends[side], coeff, consts, held))
        else:
            upper = last(plan, 0, ends[0], coeff, consts, None)
            phi = last(plan, 1, ends[1], coeff, consts, upper)

    grads = []
    for way in range(2):
        main = sum(main_sums[way]).reshape(2, 6, depth, 2, 4).sum(axis=4)
        extra = sum(extra_sums[way]).reshape(6, depth, 2, 2, 2).sum(axis=3)
        grads.append(main.transpose(2, 1, 0, 3) + extra.transpose(1, 0, 3, 2))
    sums = jnp.stack(grads, axis=1).reshape(shards, cells * 12 * bands) * (1.0 / width)
    grad = exchange(tie(sums, back[-1][-1], upper)).sum(axis=0).reshape(cells, 12, bands)
    return (phi, grad)


def solution(mesh):
    in_specs = (
        P("gx", "ba", None, None),
        P("gx", None, None),
        P(None, None, None, "gx", None),
        P("ba"),
        P("ba"),
        P("ba"),
    )
    out_specs = (P("gx", "ba", None, None), P("gx", None, "ba"))
    return jax.shard_map(body, mesh=mesh, in_specs=in_specs, out_specs=out_specs, check_vma=False)
```

```python
import functools
import math

import jax
import jax.numpy as jnp
import ml_dtypes
import numpy as np
from jax import lax
from jax.experimental import pallas as pl
from jax.experimental.pallas import tpu as pltpu
from jax.sharding import PartitionSpec as P

LANES = 128
VMEM = 56 * 1024 * 1024
CHUNK_ROWS = 16


def split_host(table):
    high = table.astype(ml_dtypes.bfloat16)
    low = (table - high.astype(np.float64)).astype(ml_dtypes.bfloat16)
    return high, low


def tables(count):
    half = count // 2
    index = np.arange(count)
    angle = (np.outer(index, index) % count) * (2.0 * np.pi / count)
    cos, sin = np.cos(angle) / math.sqrt(count), np.sin(angle) / math.sqrt(count)
    alternate = np.where(index % 2 == 0, 1.0, -1.0) / math.sqrt(count)
    into = np.concatenate([cos[:, :half], alternate[:, None], -sin[:, 1:half]], axis=1)
    weight = np.where(np.arange(half) == 0, 1.0, 2.0)[:, None]
    back = np.concatenate([weight * cos[:half], alternate[None], -2.0 * sin[1:half]], axis=0) / 12.0
    stacked = np.concatenate([cos, sin], axis=0)
    beside = np.concatenate([cos, sin], axis=1)
    return [part for table in (into, stacked, beside, back) for part in split_host(table)]


def quadrature():
    level = np.arange(6)
    polar = 0.2 + 0.15 * level
    cosine = np.concatenate([-polar, polar])
    azimuth = np.concatenate([level * (np.pi / 3.0) + np.pi / 6.0, level * (np.pi / 3.0)])
    sine = np.sqrt(1.0 - cosine * cosine)
    return (cosine, sine * np.cos(azimuth), sine * np.sin(azimuth))


def split(value):
    high = value.astype(jnp.bfloat16)
    low = (value - high.astype(jnp.float32)).astype(jnp.bfloat16)
    return high, low


def dot(left, right):
    return jnp.dot(left, right, preferred_element_type=jnp.float32)


def dot3(left, right):
    return dot(left[0], right[0]) + (dot(left[0], right[1]) + dot(left[1], right[0]))


class Plan:
    def __init__(self, shards, cells, width, rows):
        self.shards, self.cells, self.width, self.rows = shards, cells, width, rows
        self.half = width // 2
        self.chunk = min(CHUNK_ROWS, rows)
        self.chunks = rows // self.chunk
        self.tiles = self.chunk // 4
        self.main = 4 * self.chunk
        self.depth = shards * cells
        self.edge = cells * self.main
        self.pad = (cells + 7) // 8 * 8

    def height(self, chunk):
        return self.edge + (self.pad if chunk == 0 else 0)

    def shapes(self, chunk, sides):
        return [jax.ShapeDtypeStruct((self.shards, 2 // sides * self.height(chunk), LANES), jnp.float32)] * sides

    def sides_sent(self, chunk):
        return 2 if chunk == 0 else 1

    def sides_back(self, chunk):
        return 2 if chunk == self.chunks - 1 else 1

    def steps(self, chunk):
        return self.tiles + (1 if chunk == 0 else 0)


class View:
    def __init__(self, ref, offset=0):
        self.ref, self.offset = ref, offset

    def moved(self, rows):
        return pl.ds(self.offset + rows.start, rows.size, stride=rows.stride)

    def at(self, shard, rows):
        return self.ref[shard, self.moved(rows), :]

    def put(self, shard, rows, value):
        self.ref[shard, self.moved(rows), :] = value


def views(plan, at, refs):
    if len(refs) == 2:
        return [View(ref) for ref in refs]
    return [View(refs[0], side * plan.height(at)) for side in range(2)]


def forward_slabs(plan, cell, phis, into, stacked, outs):
    width, half, rows, chunk = plan.width, plan.half, plan.rows, plan.chunk
    lane = lax.broadcasted_iota(jnp.int32, (width, half), 1)
    first = lane == 0
    columns = jnp.zeros((width, half), jnp.float32)
    for band in range(2):
        packed = dot3(split(phis(band)), into)
        both = dot3(stacked, split(packed))
        cos_re, cos_im = both[:width, :half], both[:width, half:]
        sin_re, sin_im = both[width:, :half], both[width:, half:]
        real = cos_re + jnp.where(first, 0.0, sin_im)
        imag = jnp.where(first, 0.0, cos_im) - sin_re
        for at in range(plan.chunks):
            base = pl.multiple_of(cell * plan.main, 8) if at == 0 else 0
            for shard in range(plan.shards):
                start = shard * rows + at * chunk
                outs[at][shard, pl.ds(base + band * chunk, chunk), :] = real[start : start + chunk]
                outs[at][shard, pl.ds(base + (2 + band) * chunk, chunk), :] = imag[start : start + chunk]
        columns = jnp.where(lane == band, pltpu.roll(cos_im, band, 1) if band else cos_im, columns)
        columns = jnp.where(lane == band + 2, -pltpu.roll(sin_im, band + 2, 1), columns)
    turned = columns.T[:8]
    slot = lax.broadcasted_iota(jnp.int32, (1, LANES), 1)
    for shard in range(plan.shards):
        start = shard * rows
        piece = turned[:, start // LANES * LANES : start // LANES * LANES + LANES]
        row = jnp.zeros((1, LANES), jnp.float32)
        for group in range(4):
            shift = (group * rows - start) % LANES
            held = pltpu.roll(piece, shift, 1) if shift else piece
            row = jnp.where((slot >= group * rows) & (slot < (group + 1) * rows), held[group : group + 1], row)
        outs[0][shard, pl.ds(plan.edge + cell, 1), :] = row


def inverse_slabs(plan, cell, ins, beside, back, take):
    width, half, rows, chunk = plan.width, plan.half, plan.rows, plan.chunk
    lines = [ins[0][shard, pl.ds(plan.edge + cell, 1), :] for shard in range(plan.shards)]
    lines.append(jnp.zeros((LANES - plan.shards, LANES), jnp.float32))
    turned = jnp.concatenate(lines, axis=0).T[: 4 * rows]
    shifted = [pltpu.roll(turned, LANES - shard, 1) if shard else turned for shard in range(plan.shards)]
    sides = [jnp.concatenate([held[g * rows : (g + 1) * rows] for held in shifted], axis=0) for g in range(4)]
    first = lax.broadcasted_iota(jnp.int32, (width, half), 1) == 0
    uppers, lowers = [], []
    for band in range(2):
        reals, imags = [], []
        for shard in range(plan.shards):
            for at in range(plan.chunks):
                base = pl.multiple_of(cell * plan.main, 8) if at == 0 else 0
                reals.append(ins[at][shard, pl.ds(base + band * chunk, chunk), :])
                imags.append(ins[at][shard, pl.ds(base + (2 + band) * chunk, chunk), :])
        real, imag = jnp.concatenate(reals, axis=0), jnp.concatenate(imags, axis=0)
        uppers += [real, jnp.where(first, sides[band], imag)]
        lowers += [-imag, jnp.where(first, -sides[band + 2], real)]
    pairs = jnp.concatenate([jnp.concatenate(uppers, axis=1), jnp.concatenate(lowers, axis=1)], axis=0)
    mixed = dot3(beside, split(pairs))
    out = dot3(split(jnp.concatenate([mixed[:, :width], mixed[:, width:]], axis=0)), back)
    for band in range(2):
        take(band, out[band * width : (band + 1) * width])


def first_kernel(plan, kept, phi, into_h, into_l, stacked_h, stacked_l, *refs):
    cell = pl.program_id(0)
    outs = refs[kept:]
    into, stacked = (into_h[...], into_l[...]), (stacked_h[...], stacked_l[...])
    forward_slabs(plan, cell, lambda band: phi[0, band], into, stacked, outs)


def middle_kernel(plan, kept, *refs):
    cell = pl.program_id(0)
    ins = refs[: plan.chunks]
    coeff = refs[plan.chunks]
    into_h, into_l, stacked_h, stacked_l, beside_h, beside_l, back_h, back_l = refs[plan.chunks + 1 : plan.chunks + 9]
    outs, held = refs[plan.chunks + 9 + kept : -1], refs[-1]

    def take(band, value):
        held[band] = value * coeff[0]

    inverse_slabs(plan, cell, ins, (beside_h[...], beside_l[...]), (back_h[...], back_l[...]), take)
    into, stacked = (into_h[...], into_l[...]), (stacked_h[...], stacked_l[...])
    forward_slabs(plan, cell, lambda band: held[band], into, stacked, outs)


def last_kernel(plan, *refs):
    ins = refs[: plan.chunks]
    coeff, beside_h, beside_l, back_h, back_l = refs[plan.chunks : plan.chunks + 5]
    out = refs[-1]

    def take(band, value):
        out[0, band] = value * coeff[0]

    inverse_slabs(plan, pl.program_id(0), ins, (beside_h[...], beside_l[...]), (back_h[...], back_l[...]), take)


def whole(array):
    rank = len(array.shape)
    return pl.BlockSpec(array.shape, lambda cell: (0,) * rank)


def piece_specs(plan, side, sides):
    specs = []
    for at in range(plan.chunks):
        merged = sides(at) == 1
        if at == 0:
            shape = (plan.shards, plan.height(0), LANES)
            specs.append(pl.BlockSpec(shape, lambda cell, first=side if merged else 0: (0, first, 0)))
        else:
            shape = (plan.shards, plan.main, LANES)
            specs.append(pl.BlockSpec(shape, lambda cell, first=side * plan.cells if merged else 0: (0, first + cell, 0)))
    return specs


def sent_shapes(plan):
    return [plan.shapes(at, plan.sides_sent(at))[0] for at in range(plan.chunks)]


def slab_spec(plan, side):
    return pl.BlockSpec((1, 2, plan.width, plan.width), lambda cell: (cell, side, 0, 0))


def coeff_spec(plan):
    return pl.BlockSpec((1, plan.width, plan.width), lambda cell: (cell, 0, 0))


def cost(microseconds):
    return pl.CostEstimate(flops=0, bytes_accessed=int(microseconds * 3.69e6), transcendentals=0)


PARAMS = pltpu.CompilerParams(vmem_limit_bytes=VMEM)


def send(kernel, plan, side, operands, in_specs, held, microseconds, scratch, name):
    aliases = {}
    for at in range(plan.chunks):
        if held is not None and plan.sides_sent(at) == 1:
            aliases[len(operands)] = at
            operands, in_specs = operands + [held[at]], in_specs + [pl.BlockSpec(memory_space=pl.ANY)]
    return pl.pallas_call(
        functools.partial(kernel, plan, len(aliases)),
        grid=(plan.cells,),
        in_specs=in_specs,
        out_specs=piece_specs(plan, side, plan.sides_sent),
        out_shape=sent_shapes(plan),
        input_output_aliases=aliases,
        scratch_shapes=scratch,
        compiler_params=PARAMS,
        cost_estimate=cost(microseconds),
        name=name,
    )(*operands)


def first(plan, side, phi, consts, held):
    in_specs = [slab_spec(plan, side)] + [whole(c) for c in consts[:4]]
    return send(first_kernel, plan, side, [phi, *consts[:4]], in_specs, held, 12, [], "into_modes")


def middle(plan, side, ins, coeff, consts, held):
    in_specs = piece_specs(plan, side, plan.sides_back) + [coeff_spec(plan)] + [whole(c) for c in consts]
    scratch = [pltpu.VMEM((2, plan.width, plan.width), jnp.float32)]
    return send(middle_kernel, plan, side, [*ins, coeff, *consts], in_specs, held, 25, scratch, "between_steps")


def last(plan, side, ins, coeff, consts, held):
    operands = [*ins, coeff, *consts[4:]]
    in_specs = piece_specs(plan, side, plan.sides_back) + [coeff_spec(plan)] + [whole(c) for c in consts[4:]]
    aliases = {}
    if held is not None:
        aliases = {len(operands): 0}
        operands.append(held)
        in_specs.append(pl.BlockSpec(memory_space=pl.ANY))
    return pl.pallas_call(
        functools.partial(last_kernel, plan),
        grid=(plan.cells,),
        in_specs=in_specs,
        out_specs=slab_spec(plan, side),
        out_shape=jax.ShapeDtypeStruct((plan.cells, 4, plan.width, plan.width), jnp.float32),
        input_output_aliases=aliases,
        compiler_params=PARAMS,
        cost_estimate=cost(16),
        name="out_of_modes",
    )(*operands)


def sweep_kernel(plan, at, upward, groups, *refs):
    refs = list(refs)

    def pop(count):
        taken = refs[:count]
        del refs[:count]
        return taken

    specs = views(plan, at, pop(plan.sides_sent(at)))
    aims, inv, couple, rate = pop(4)
    if upward:
        parts = views(plan, at, pop(2))
        extras = pop(1)[0] if at == 0 else None
        share, keep = pop(2)
        fluxes = pop(groups)
        outs = views(plan, at, pop(plan.sides_back(at)))
        sums, totals = refs
    else:
        outs = views(plan, at, pop(2))
        flux, sums = pop(2)
        extras = pop(1)[0] if at == 0 else None
        totals = refs[0]
    tiles, depth, cells, main, rows = plan.tiles, plan.depth, plan.cells, plan.main, plan.rows
    imag_at = 2 * plan.chunk
    sub = lax.broadcasted_iota(jnp.int32, (8, LANES), 0)
    lane = lax.broadcasted_iota(jnp.int32, (1, LANES), 1)
    zeros = jnp.zeros((8, LANES), jnp.float32)
    cosine = [abs(float(c)) / 12.0 for c in quadrature()[0][:6]]

    def place(cell, base, tile):
        return pl.ds(cell * main + base + tile, 8, stride=tiles)

    def extra_source(shard, cell, base):
        edge = []
        for s in range(2):
            line = specs[s].at(shard, pl.ds(plan.edge + cell, 1))
            line = pltpu.roll(line, LANES - 2 * rows, 1) if base else line
            edge.append(jnp.where(sub < 4, line, pltpu.roll(line, LANES - rows, 1)))
        row0 = [specs[s].at(shard, place(cell, base, 0)) for s in range(2)]
        kind = sub % 4
        value = jnp.where(kind == 0, row0[0], jnp.where(kind == 1, pltpu.roll(row0[1], 1, 0), 0.0))
        return jnp.where(kind == 2, edge[0], jnp.where(kind == 3, edge[1], value))

    def extra_store(shard, cell, new_re, new_im):
        if not upward:
            extras[shard * cells + cell, 0] = new_re
            extras[shard * cells + cell, 1] = new_im
            return
        new_re = new_re + extras[shard * cells + cell, 0]
        new_im = new_im + extras[shard * cells + cell, 1]
        spread = [new_re, pltpu.roll(new_re, rows, 1), pltpu.roll(new_im, 2 * rows, 1), pltpu.roll(new_im, 3 * rows, 1)]
        for side in range(2):
            row = spread[0][2 + side : 3 + side]
            for group in range(1, 4):
                at_sub = 2 + side + 4 * (group % 2)
                row = jnp.where(lane < group * rows, row, spread[group][at_sub : at_sub + 1])
            outs[side].put(shard, pl.ds(plan.edge + cell, 1), row)
            for base, value in ((0, new_re), (imag_at, new_im)):
                value = pltpu.roll(value, 7, 0) if side else value
                held = outs[side].at(shard, place(cell, base, 0))
                pair = (sub % 4 == 0) & (keep[...] > 0.0)
                outs[side].put(shard, place(cell, base, 0), jnp.where(pair, 0.5 * (held + value), held))

    for count in range(2 * tiles + (1 if at == 0 else 0)):
        extra = count == 2 * tiles
        side, tile = (2, tiles) if extra else (count // tiles, count % tiles)
        inv_re = [inv[0, d, count] for d in range(6)]
        inv_im = [inv[1, d, count] for d in range(6)]
        fresh = extra or tile == 0

        def block(step, psi, extra=extra, side=side, tile=tile, inv_re=inv_re, inv_im=inv_im, fresh=fresh):
            psi_re, psi_im = list(psi[:6]), list(psi[6:])
            shard = step if upward else plan.shards - 1 - step
            for cell in range(cells) if upward else range(cells - 1, -1, -1):
                z = shard * cells + cell
                if extra:
                    row_re, row_im = extra_source(shard, cell, 0), extra_source(shard, cell, imag_at)
                else:
                    row_re = specs[side].at(shard, place(cell, 0, tile))
                    row_im = specs[side].at(shard, place(cell, imag_at, tile))
                row_re, row_im = rate[side] * row_re, rate[side] * row_im
                aim_re, aim_im = aims[z, 0, tile], aims[z, 1, tile]
                for d in range(6):
                    sum_re = row_re + couple[side, d] * psi_re[d]
                    sum_im = row_im + couple[side, d] * psi_im[d]
                    psi_re[d] = inv_re[d] * sum_re - inv_im[d] * sum_im
                    psi_im[d] = inv_re[d] * sum_im + inv_im[d] * sum_re
                    product = psi_re[d] * aim_re + psi_im[d] * aim_im
                    totals[side, d, z] = product if fresh else totals[side, d, z] + product
                new_re = ((psi_re[0] + psi_re[1]) + (psi_re[2] + psi_re[3])) + (psi_re[4] + psi_re[5])
                new_im = ((psi_im[0] + psi_im[1]) + (psi_im[2] + psi_im[3])) + (psi_im[4] + psi_im[5])
                if extra:
                    extra_store(shard, cell, new_re, new_im)
                    continue
                if upward:
                    new_re = new_re + parts[side].at(shard, place(cell, 0, tile))
                    new_im = new_im + parts[side].at(shard, place(cell, imag_at, tile))
                outs[side].put(shard, place(cell, 0, tile), new_re)
                outs[side].put(shard, place(cell, imag_at, tile), new_im)
            return tuple(psi_re + psi_im)

        if upward:
            start = []
            for part in range(2):
                value = fluxes[0][part, tile]
                for other in fluxes[1:]:
                    value = value + other[part, tile]
                start += [share[side] * value] * 6
        else:
            start = [zeros] * 12
        carried = lax.fori_loop(0, plan.shards, block, tuple(start))
        if not upward:
            for part in range(2):
                value = carried[6 * part] * cosine[0]
                for d in range(1, 6):
                    value = value + carried[6 * part + d] * cosine[d]
                value = value + pltpu.roll(value, 4, 0)
                if extra:
                    swapped = jnp.where(sub % 2 == 0, pltpu.roll(value, 7, 0), pltpu.roll(value, 1, 0))
                    flux[part, tile] = value + swapped
                elif side == 0:
                    flux[part, tile] = value
                else:
                    flux[part, tile] = flux[part, tile] + value
    for side in range(3 if at == 0 else 2):
        for d in range(6):
            sums[side, d] = jnp.sum(totals[side, d], axis=-1)


def sweep(plan, at, upward, groups, *operands):
    tiles = plan.steps(at)
    sides = 3 if at == 0 else 2
    vmem = pl.BlockSpec(memory_space=pltpu.VMEM)
    out_shape = plan.shapes(at, plan.sides_back(at) if upward else 2)
    if not upward:
        out_shape.append(jax.ShapeDtypeStruct((2, tiles, 8, LANES), jnp.float32))
    out_shape.append(jax.ShapeDtypeStruct((sides, 6, plan.depth, 8), jnp.float32))
    if not upward and at == 0:
        out_shape.append(jax.ShapeDtypeStruct((plan.depth, 2, 8, LANES), jnp.float32))
    return pl.pallas_call(
        functools.partial(sweep_kernel, plan, at, upward, groups),
        in_specs=[vmem] * len(operands),
        out_specs=[vmem] * len(out_shape),
        out_shape=out_shape,
        scratch_shapes=[pltpu.VMEM((sides, 6, plan.depth, 8, LANES), jnp.float32)],
        compiler_params=PARAMS,
        cost_estimate=cost(13),
        name="upward" if upward else "downward",
    )(*operands)


def mirror_kernel(plan, group, upper, lanes_turned, rows_turned, turned, lead):
    rows, half = plan.rows, plan.half
    cells = upper.shape[1]
    for part in range(2):
        sign = 1.0 if part == 0 else -1.0
        pairs = split(sign * upper[part].reshape(cells * rows, half))
        value = dot(pairs[0], lanes_turned[...]) + dot(pairs[1], lanes_turned[...])
        lead[part] = value.reshape(cells, rows, half)[:, 0, :]
        pairs = split(value)
        value = dot(rows_turned[...], pairs[0]) + dot(rows_turned[...], pairs[1])
        turned[part] = value.reshape(cells, rows, half)


def mirror(plan, forward, groups):
    cells = 8
    rows, half = plan.rows, plan.half
    share = plan.depth // groups
    lanes_turned = np.zeros((half, half), ml_dtypes.bfloat16)
    rows_turned = np.zeros((cells * rows, cells * rows), ml_dtypes.bfloat16)
    for k in range(1, half):
        lanes_turned[half - k, k] = 1
    for c in range(cells):
        for r in range(1, rows):
            rows_turned[c * rows + r, c * rows + rows - r] = 1
    lanes_turned, rows_turned = jnp.asarray(lanes_turned), jnp.asarray(rows_turned)
    blocks = share // cells
    group = lax.axis_index("ba").astype(jnp.int32).reshape(1)
    spec = pltpu.PrefetchScalarGridSpec(
        num_scalar_prefetch=1,
        grid=(forward.shape[0], blocks),
        in_specs=[
            pl.BlockSpec((None, 2, cells, rows, half), lambda step, z, at: (step, 0, at[0] * blocks + z, 0, 1)),
            pl.BlockSpec(lanes_turned.shape, lambda step, z, at: (0, 0)),
            pl.BlockSpec(rows_turned.shape, lambda step, z, at: (0, 0)),
        ],
        out_specs=[
            pl.BlockSpec((None, 2, cells, rows, half), lambda step, z, at: (step, 0, z, 0, 0)),
            pl.BlockSpec((None, 2, cells, half), lambda step, z, at: (step, 0, z, 0)),
        ],
    )
    return pl.pallas_call(
        functools.partial(mirror_kernel, plan),
        grid_spec=spec,
        out_shape=[
            jax.ShapeDtypeStruct((forward.shape[0], 2, share, rows, half), jnp.float32),
            jax.ShapeDtypeStruct((forward.shape[0], 2, share, half), jnp.float32),
        ],
        compiler_params=PARAMS,
        cost_estimate=cost(5),
        name="mirrored",
    )(group, forward, lanes_turned, rows_turned)


def aims_kernel(plan, at, group, own, other, keep, out, held):
    half, chunk, tiles = plan.half, plan.chunk, plan.tiles
    cells, rows = own.shape[1:3]
    row = lax.broadcasted_iota(jnp.int32, (chunk, half), 0)
    sub = lax.broadcasted_iota(jnp.int32, (8, LANES), 0)
    lane = lax.broadcasted_iota(jnp.int32, (1, LANES), 1)
    for part in range(2):
        if at == 0:
            owner = keep[...] > 0.0
            line = own[part, :, :, half:].reshape(cells * rows, half).T[:1]
            if cells * rows < LANES:
                line = jnp.concatenate([line, jnp.zeros((1, LANES - cells * rows), jnp.float32)], axis=1)
        for cell in range(cells):
            mine, theirs = own[part, cell, :chunk, :half], other[part, cell]
            if at == 0:
                held[...] = mine + jnp.where((row == 0) & owner[:1], 0.0, theirs)
            else:
                held[...] = mine + theirs
            for tile in range(tiles):
                four = held[pl.ds(tile, 4, stride=tiles), :]
                out[cell, part, tile] = jnp.concatenate([four, four], axis=0)
            if at == 0:
                partner = jnp.where(owner, theirs[:1], 0.0)
                start = cell * rows
                piece = line[:, start // LANES * LANES : start // LANES * LANES + LANES]
                at_zero = pltpu.roll(piece, LANES - start % LANES, 1) if start % LANES else piece
                out[cell, part, tiles] = jnp.where(sub % 4 < 2, partner, jnp.where(lane < rows, at_zero, 0.0))


def make_aims(plan, at, own, parts, keep, step):
    cells = 8
    half, chunk = plan.half, plan.chunk
    other = jnp.stack(parts)
    groups = other.shape[0]
    blocks = other.shape[2] // cells
    group = lax.axis_index("ba").astype(jnp.int32).reshape(1)
    own_rows = plan.rows if at == 0 else chunk

    def sender(z, me):
        return (lax.rem(me[0] + groups - z // blocks, groups), 0, z % blocks, 0, 0)

    spec = pltpu.PrefetchScalarGridSpec(
        num_scalar_prefetch=1,
        grid=(plan.depth // cells,),
        in_specs=[
            pl.BlockSpec((None, 2, cells, own_rows, plan.width), lambda z, me: (step, 0, z, at, 0)),
            pl.BlockSpec((None, 2, cells, chunk, half), sender),
            pl.BlockSpec(keep.shape, lambda z, me: (0, 0)),
        ],
        out_specs=pl.BlockSpec((cells, 2, plan.steps(at), 8, LANES), lambda z, me: (z, 0, 0, 0, 0)),
        scratch_shapes=[pltpu.VMEM((chunk, half), jnp.float32)],
    )
    return pl.pallas_call(
        functools.partial(aims_kernel, plan, at),
        grid_spec=spec,
        out_shape=jax.ShapeDtypeStruct((plan.depth, 2, plan.steps(at), 8, LANES), jnp.float32),
        compiler_params=PARAMS,
        cost_estimate=cost(4),
        name="targets",
    )(group, own, other, keep)


def lift(value):
    main = jnp.broadcast_to(value.reshape(2, 2, 1), (2, 2, 4)).reshape(2, 8)
    extra = jnp.broadcast_to(value.reshape(2, 2).T[:, None, :], (2, 2, 2)).reshape(1, 8)
    return jnp.broadcast_to(jnp.concatenate([main, extra])[:, :, None], (3, 8, LANES))


def factors(plan, at, place, rate, speed):
    unit = 1.5 * 2.0 * math.pi / plan.width
    half, width, tiles = plan.half, plan.width, plan.tiles
    base = place * plan.rows
    sub = jnp.arange(8)

    def signed(index):
        return ((index + half) % width - half).astype(jnp.float32) * unit

    row = base + at * plan.chunk + jnp.arange(tiles)[:, None] + tiles * (sub % 4)[None, :]
    freq_x = jnp.broadcast_to(signed(row)[None, :, :, None], (2, tiles, 8, LANES)).reshape(2 * tiles, 8, LANES)
    freq_y = jnp.broadcast_to(signed(jnp.arange(LANES)), (2 * tiles, 8, LANES))
    sides = [0] * tiles + [1] * tiles
    if at == 0:
        partner = (sub % 4 < 2)[:, None]
        extra_x = jnp.where(partner, -signed(base), signed(base + jnp.arange(LANES) % plan.rows)[None, :])
        extra_y = jnp.where(partner, signed(jnp.arange(LANES))[None, :], signed(jnp.asarray(half)))
        freq_x = jnp.concatenate([freq_x, extra_x[None]], axis=0)
        freq_y = jnp.concatenate([freq_y, extra_y[None]], axis=0)
        sides.append(2)
    rate, speed = [jnp.concatenate([v[s : s + 1] for s in sides]) for v in (rate, speed)]
    cosine, along_x, along_y = [np.asarray(q, np.float32).reshape(12, 1, 1, 1) for q in quadrature()]
    wave = speed * (along_x * freq_x + along_y * freq_y)
    real = rate + np.abs(cosine) * speed
    denom = real * real + wave * wave
    return jnp.stack([real / denom, -wave / denom])


def body(phi_start, coeff, forward, rates, speeds, shares):
    shards = lax.axis_size("gx")
    groups = lax.axis_size("ba")
    place = lax.axis_index("gx")
    cells, bands, width, _ = phi_start.shape
    rows = forward.shape[3]
    steps = forward.shape[0]
    plan = Plan(shards, cells, width, rows)
    depth = plan.depth
    consts = [jnp.asarray(part) for part in tables(width)]
    owner = place * rows == plan.half
    keep = jnp.broadcast_to(jnp.where(owner, 1.0, 0.0).astype(jnp.float32), (8, LANES))
    rate, speed, share = lift(rates), lift(speeds), lift(shares)
    polar = np.abs(np.asarray(quadrature()[0][:6], np.float32)).reshape(1, 6, 1, 1)
    couple = polar * speed[:, None]
    inverse = [factors(plan, at, place, rate, speed) for at in range(plan.chunks)]

    def tie(value, *others):
        return lax.optimization_barrier((value, *others))[0]

    def swap_targets(turned, lead):
        turned = lax.ppermute(turned, "gx", [(i, shards - 1 - i) for i in range(shards)])
        lead = lax.ppermute(lead, "gx", [(i, (shards - i) % shards) for i in range(shards)])
        return jnp.where(jnp.arange(rows)[:, None] == 0, lead[:, :, :, None, :], turned)

    def spread_targets(turned):
        parts = [turned]
        for shift in range(1, groups):
            parts.append(lax.ppermute(turned, "ba", [(i, (i + shift) % groups) for i in range(groups)]))
        return parts

    def exchange(array):
        return lax.all_to_all(array, "gx", split_axis=0, concat_axis=0, tiled=True)

    main_sums, extra_sums = [[], []], [[], []]

    def collect(sums, way):
        main_sums[way].append(sums[:2])
        if sums.shape[0] == 3:
            extra_sums[way].append(sums[2])

    def into(transform):
        pieces, held = [[] for _ in range(plan.chunks)], None
        for side in range(2):
            held = transform(side, held)
            for at in range(plan.chunks):
                if plan.sides_sent(at) == 2 or side == 1:
                    pieces[at].append(held[at])
        return pieces

    def in_order(pieces, after, besides=()):
        arrived = []
        for piece in pieces:
            if after is not None:
                piece = tie(piece, after, *besides)
            after = exchange(piece)
            arrived.append(after)
        return arrived

    flipped = mirror(plan, forward, groups)
    swapped = swap_targets(*flipped)
    starts = [tie(phi_start, *flipped), tie(phi_start, swapped)]
    sent = into(lambda side, held: first(plan, side, starts[side], consts, held))
    chunk_rows = [slice(at * plan.chunk, (at + 1) * plan.chunk) for at in range(plan.chunks)]
    spread = [[spread_targets(swapped[step][:, :, held]) for held in chunk_rows] for step in range(steps)]
    for step in range(steps):
        modes, after = [], None
        for at in range(plan.chunks):
            modes.append(in_order(sent[at], after, spread[0][at] if step == 0 else ()))
            after = modes[at][-1]
        back = []
        back = []
        for at in range(plan.chunks):
            inv = inverse[at]
            common = (*modes[at], make_aims(plan, at, forward, spread[step][at], keep, step))
            part0, part1, flux, sums, *extras = sweep(plan, at, False, groups, *common, inv[:, :6], couple, rate)
            collect(sums, 0)
            fluxes = [flux]
            for shift in range(1, groups):
                fluxes.append(lax.ppermute(flux, "ba", [(i, (i + shift) % groups) for i in range(groups)]))
            rest = (part0, part1, *extras, share, keep, *fluxes)
            *new, sums = sweep(plan, at, True, groups, *common, inv[:, 6:], couple, rate, *rest)
            collect(sums, 1)
            if step + 1 < steps and at == plan.chunks - 1:
                for part, parts in enumerate(spread[step + 1]):
                    new[part % len(new)] = tie(new[part % len(new)], *parts)
            back.append(in_order(new, back[-1][-1] if back else None))
        ends = [[pieces[side % len(pieces)] for pieces in back] for side in range(2)]
        if step + 1 < steps:
            sent = into(lambda side, held: middle(plan, side, ends[side], coeff, consts, held))
        else:
            upper = last(plan, 0, ends[0], coeff, consts, None)
            phi = last(plan, 1, ends[1], coeff, consts, upper)

    grads = []
    for way in range(2):
        main = sum(main_sums[way]).reshape(2, 6, depth, 2, 4).sum(axis=4)
        extra = sum(extra_sums[way]).reshape(6, depth, 2, 2, 2).sum(axis=3)
        grads.append(main.transpose(2, 1, 0, 3) + extra.transpose(1, 0, 3, 2))
    sums = jnp.stack(grads, axis=1).reshape(shards, cells * 12 * bands) * (1.0 / width)
    grad = exchange(tie(sums, back[-1][-1], upper)).sum(axis=0).reshape(cells, 12, bands)
    return (phi, grad)


def solution(mesh):
    in_specs = (
        P("gx", "ba", None, None),
        P("gx", None, None),
        P(None, None, None, "gx", None),
        P("ba"),
        P("ba"),
        P("ba"),
    )
    out_specs = (P("gx", "ba", None, None), P("gx", None, "ba"))
    return jax.shard_map(body, mesh=mesh, in_specs=in_specs, out_specs=out_specs, check_vma=False)
```

```python
import functools
import math

import jax
import jax.numpy as jnp
import ml_dtypes
import numpy as np
from jax import lax
from jax.experimental import pallas as pl
from jax.experimental.pallas import tpu as pltpu
from jax.sharding import PartitionSpec as P

LANES = 128
VMEM = 56 * 1024 * 1024
CHUNK_ROWS = 16


def split_host(table):
    high = table.astype(ml_dtypes.bfloat16)
    low = (table - high.astype(np.float64)).astype(ml_dtypes.bfloat16)
    return high, low


def tables(count):
    half = count // 2
    index = np.arange(count)
    angle = (np.outer(index, index) % count) * (2.0 * np.pi / count)
    cos, sin = np.cos(angle) / math.sqrt(count), np.sin(angle) / math.sqrt(count)
    alternate = np.where(index % 2 == 0, 1.0, -1.0) / math.sqrt(count)
    into = np.concatenate([cos[:, :half], alternate[:, None], -sin[:, 1:half]], axis=1)
    weight = np.where(np.arange(half) == 0, 1.0, 2.0)[:, None]
    back = np.concatenate([weight * cos[:half], alternate[None], -2.0 * sin[1:half]], axis=0) / 12.0
    stacked = np.concatenate([cos, sin], axis=0)
    beside = np.concatenate([cos, sin], axis=1)
    return [part for table in (into, stacked, beside, back) for part in split_host(table)]


def quadrature():
    level = np.arange(6)
    polar = 0.2 + 0.15 * level
    cosine = np.concatenate([-polar, polar])
    azimuth = np.concatenate([level * (np.pi / 3.0) + np.pi / 6.0, level * (np.pi / 3.0)])
    sine = np.sqrt(1.0 - cosine * cosine)
    return (cosine, sine * np.cos(azimuth), sine * np.sin(azimuth))


def split(value):
    high = value.astype(jnp.bfloat16)
    low = (value - high.astype(jnp.float32)).astype(jnp.bfloat16)
    return high, low


def dot(left, right):
    return jnp.dot(left, right, preferred_element_type=jnp.float32)


def dot3(left, right):
    return dot(left[0], right[0]) + (dot(left[0], right[1]) + dot(left[1], right[0]))


class Plan:
    def __init__(self, shards, cells, width, rows):
        self.shards, self.cells, self.width, self.rows = shards, cells, width, rows
        self.half = width // 2
        self.chunk = min(CHUNK_ROWS, rows)
        self.chunks = rows // self.chunk
        self.tiles = self.chunk // 4
        self.main = 4 * self.chunk
        self.depth = shards * cells
        self.edge = cells * self.main
        self.batch = 4 if cells % 4 == 0 else 2 if cells % 2 == 0 else 1
        self.pad = (cells + 7) // 8 * 8

    def height(self, chunk):
        return self.edge + (self.pad if chunk == 0 else 0)

    def shapes(self, chunk, sides):
        return [jax.ShapeDtypeStruct((self.shards, 2 // sides * self.height(chunk), LANES), jnp.float32)] * sides

    def sides_sent(self, chunk):
        return 2 if chunk == 0 else 1

    def sides_back(self, chunk):
        return 2 if chunk == self.chunks - 1 else 1

    def steps(self, chunk):
        return self.tiles + (1 if chunk == 0 else 0)


class View:
    def __init__(self, ref, offset=0):
        self.ref, self.offset = ref, offset

    def moved(self, rows):
        return pl.ds(self.offset + rows.start, rows.size, stride=rows.stride)

    def at(self, shard, rows):
        return self.ref[shard, self.moved(rows), :]

    def put(self, shard, rows, value):
        self.ref[shard, self.moved(rows), :] = value


def views(plan, at, refs):
    if len(refs) == 2:
        return [View(ref) for ref in refs]
    return [View(refs[0], side * plan.height(at)) for side in range(2)]


def forward_slabs(plan, step, phis, into, stacked, outs):
    for sub in range(plan.batch):
        forward_cell(plan, step * plan.batch + sub, sub, functools.partial(phis, sub), into, stacked, outs)


def forward_cell(plan, cell, sub, phis, into, stacked, outs):
    width, half, rows, chunk = plan.width, plan.half, plan.rows, plan.chunk
    lane = lax.broadcasted_iota(jnp.int32, (width, half), 1)
    first = lane == 0
    columns = jnp.zeros((width, half), jnp.float32)
    for band in range(2):
        packed = dot3(split(phis(band)), into)
        both = dot3(stacked, split(packed))
        cos_re, cos_im = both[:width, :half], both[:width, half:]
        sin_re, sin_im = both[width:, :half], both[width:, half:]
        real = cos_re + jnp.where(first, 0.0, sin_im)
        imag = jnp.where(first, 0.0, cos_im) - sin_re
        for at in range(plan.chunks):
            base = pl.multiple_of(cell * plan.main, 8) if at == 0 else sub * plan.main
            for shard in range(plan.shards):
                start = shard * rows + at * chunk
                outs[at][shard, pl.ds(base + band * chunk, chunk), :] = real[start : start + chunk]
                outs[at][shard, pl.ds(base + (2 + band) * chunk, chunk), :] = imag[start : start + chunk]
        columns = jnp.where(lane == band, pltpu.roll(cos_im, band, 1) if band else cos_im, columns)
        columns = jnp.where(lane == band + 2, -pltpu.roll(sin_im, band + 2, 1), columns)
    turned = columns.T[:8]
    slot = lax.broadcasted_iota(jnp.int32, (1, LANES), 1)
    for shard in range(plan.shards):
        start = shard * rows
        piece = turned[:, start // LANES * LANES : start // LANES * LANES + LANES]
        row = jnp.zeros((1, LANES), jnp.float32)
        for group in range(4):
            shift = (group * rows - start) % LANES
            held = pltpu.roll(piece, shift, 1) if shift else piece
            row = jnp.where((slot >= group * rows) & (slot < (group + 1) * rows), held[group : group + 1], row)
        outs[0][shard, pl.ds(plan.edge + cell, 1), :] = row


def inverse_slabs(plan, step, ins, beside, back, take):
    width = plan.width
    uppers, lowers = [], []
    for sub in range(plan.batch):
        inverse_cell(plan, step * plan.batch + sub, sub, ins, uppers, lowers)
    pairs = jnp.concatenate([jnp.concatenate(uppers, axis=1), jnp.concatenate(lowers, axis=1)], axis=0)
    mixed = dot3(beside, split(pairs))
    slabs = [mixed[:, i * width : (i + 1) * width] for i in range(2 * plan.batch)]
    out = dot3(split(jnp.concatenate(slabs, axis=0)), back)
    for sub in range(plan.batch):
        for band in range(2):
            start = (2 * sub + band) * width
            take(sub, band, out[start : start + width])


def inverse_cell(plan, cell, sub, ins, uppers, lowers):
    width, half, rows, chunk = plan.width, plan.half, plan.rows, plan.chunk
    lines = [ins[0][shard, pl.ds(plan.edge + cell, 1), :] for shard in range(plan.shards)]
    lines.append(jnp.zeros((LANES - plan.shards, LANES), jnp.float32))
    turned = jnp.concatenate(lines, axis=0).T[: 4 * rows]
    shifted = [pltpu.roll(turned, LANES - shard, 1) if shard else turned for shard in range(plan.shards)]
    sides = [jnp.concatenate([held[g * rows : (g + 1) * rows] for held in shifted], axis=0) for g in range(4)]
    first = lax.broadcasted_iota(jnp.int32, (width, half), 1) == 0
    for band in range(2):
        reals, imags = [], []
        for shard in range(plan.shards):
            for at in range(plan.chunks):
                base = pl.multiple_of(cell * plan.main, 8) if at == 0 else sub * plan.main
                reals.append(ins[at][shard, pl.ds(base + band * chunk, chunk), :])
                imags.append(ins[at][shard, pl.ds(base + (2 + band) * chunk, chunk), :])
        real, imag = jnp.concatenate(reals, axis=0), jnp.concatenate(imags, axis=0)
        uppers += [real, jnp.where(first, sides[band], imag)]
        lowers += [-imag, jnp.where(first, -sides[band + 2], real)]


def first_kernel(plan, kept, phi, into_h, into_l, stacked_h, stacked_l, *refs):
    cell = pl.program_id(0)
    outs = refs[kept:]
    into, stacked = (into_h[...], into_l[...]), (stacked_h[...], stacked_l[...])
    forward_slabs(plan, cell, lambda sub, band: phi[sub, band], into, stacked, outs)


def middle_kernel(plan, kept, *refs):
    cell = pl.program_id(0)
    ins = refs[: plan.chunks]
    coeff = refs[plan.chunks]
    into_h, into_l, stacked_h, stacked_l, beside_h, beside_l, back_h, back_l = refs[plan.chunks + 1 : plan.chunks + 9]
    outs, held = refs[plan.chunks + 9 + kept : -1], refs[-1]

    def take(sub, band, value):
        held[sub, band] = value * coeff[sub]

    inverse_slabs(plan, cell, ins, (beside_h[...], beside_l[...]), (back_h[...], back_l[...]), take)
    into, stacked = (into_h[...], into_l[...]), (stacked_h[...], stacked_l[...])
    forward_slabs(plan, cell, lambda sub, band: held[sub, band], into, stacked, outs)


def last_kernel(plan, *refs):
    ins = refs[: plan.chunks]
    coeff, beside_h, beside_l, back_h, back_l = refs[plan.chunks : plan.chunks + 5]
    out = refs[-1]

    def take(sub, band, value):
        out[sub, band] = value * coeff[sub]

    inverse_slabs(plan, pl.program_id(0), ins, (beside_h[...], beside_l[...]), (back_h[...], back_l[...]), take)


def whole(array):
    rank = len(array.shape)
    return pl.BlockSpec(array.shape, lambda cell: (0,) * rank)


def piece_specs(plan, side, sides):
    specs = []
    for at in range(plan.chunks):
        merged = sides(at) == 1
        if at == 0:
            shape = (plan.shards, plan.height(0), LANES)
            specs.append(pl.BlockSpec(shape, lambda cell, first=side if merged else 0: (0, first, 0)))
        else:
            shape = (plan.shards, plan.batch * plan.main, LANES)
            first = side * plan.cells // plan.batch if merged else 0
            specs.append(pl.BlockSpec(shape, lambda cell, first=first: (0, first + cell, 0)))
    return specs


def sent_shapes(plan):
    return [plan.shapes(at, plan.sides_sent(at))[0] for at in range(plan.chunks)]


def slab_spec(plan, side):
    return pl.BlockSpec((plan.batch, 2, plan.width, plan.width), lambda cell: (cell, side, 0, 0))


def coeff_spec(plan):
    return pl.BlockSpec((plan.batch, plan.width, plan.width), lambda cell: (cell, 0, 0))


def cost(microseconds):
    return pl.CostEstimate(flops=0, bytes_accessed=int(microseconds * 3.69e6), transcendentals=0)


PARAMS = pltpu.CompilerParams(vmem_limit_bytes=VMEM)


def send(kernel, plan, side, operands, in_specs, held, microseconds, scratch, name):
    aliases = {}
    for at in range(plan.chunks):
        if held is not None and plan.sides_sent(at) == 1:
            aliases[len(operands)] = at
            operands, in_specs = operands + [held[at]], in_specs + [pl.BlockSpec(memory_space=pl.ANY)]
    return pl.pallas_call(
        functools.partial(kernel, plan, len(aliases)),
        grid=(plan.cells // plan.batch,),
        in_specs=in_specs,
        out_specs=piece_specs(plan, side, plan.sides_sent),
        out_shape=sent_shapes(plan),
        input_output_aliases=aliases,
        scratch_shapes=scratch,
        compiler_params=PARAMS,
        cost_estimate=cost(microseconds),
        name=name,
    )(*operands)


def first(plan, side, phi, consts, held):
    in_specs = [slab_spec(plan, side)] + [whole(c) for c in consts[:4]]
    return send(first_kernel, plan, side, [phi, *consts[:4]], in_specs, held, 12, [], "into_modes")


def middle(plan, side, ins, coeff, consts, held):
    in_specs = piece_specs(plan, side, plan.sides_back) + [coeff_spec(plan)] + [whole(c) for c in consts]
    scratch = [pltpu.VMEM((plan.batch, 2, plan.width, plan.width), jnp.float32)]
    return send(middle_kernel, plan, side, [*ins, coeff, *consts], in_specs, held, 25, scratch, "between_steps")


def last(plan, side, ins, coeff, consts, held):
    operands = [*ins, coeff, *consts[4:]]
    in_specs = piece_specs(plan, side, plan.sides_back) + [coeff_spec(plan)] + [whole(c) for c in consts[4:]]
    aliases = {}
    if held is not None:
        aliases = {len(operands): 0}
        operands.append(held)
        in_specs.append(pl.BlockSpec(memory_space=pl.ANY))
    return pl.pallas_call(
        functools.partial(last_kernel, plan),
        grid=(plan.cells // plan.batch,),
        in_specs=in_specs,
        out_specs=slab_spec(plan, side),
        out_shape=jax.ShapeDtypeStruct((plan.cells, 4, plan.width, plan.width), jnp.float32),
        input_output_aliases=aliases,
        compiler_params=PARAMS,
        cost_estimate=cost(16),
        name="out_of_modes",
    )(*operands)


def sweep_kernel(plan, at, upward, groups, *refs):
    refs = list(refs)

    def pop(count):
        taken = refs[:count]
        del refs[:count]
        return taken

    specs = views(plan, at, pop(plan.sides_sent(at)))
    aims, inv, couple, rate = pop(4)
    if upward:
        parts = views(plan, at, pop(2))
        extras = pop(1)[0] if at == 0 else None
        share, keep = pop(2)
        fluxes = pop(groups)
        outs = views(plan, at, pop(plan.sides_back(at)))
        sums, totals = refs
    else:
        outs = views(plan, at, pop(2))
        flux, sums = pop(2)
        extras = pop(1)[0] if at == 0 else None
        totals = refs[0]
    tiles, depth, cells, main, rows = plan.tiles, plan.depth, plan.cells, plan.main, plan.rows
    imag_at = 2 * plan.chunk
    sub = lax.broadcasted_iota(jnp.int32, (8, LANES), 0)
    lane = lax.broadcasted_iota(jnp.int32, (1, LANES), 1)
    zeros = jnp.zeros((8, LANES), jnp.float32)
    cosine = [abs(float(c)) / 12.0 for c in quadrature()[0][:6]]

    def place(cell, base, tile):
        return pl.ds(cell * main + base + tile, 8, stride=tiles)

    def extra_source(shard, cell, base):
        edge = []
        for s in range(2):
            line = specs[s].at(shard, pl.ds(plan.edge + cell, 1))
            line = pltpu.roll(line, LANES - 2 * rows, 1) if base else line
            edge.append(jnp.where(sub < 4, line, pltpu.roll(line, LANES - rows, 1)))
        row0 = [specs[s].at(shard, place(cell, base, 0)) for s in range(2)]
        kind = sub % 4
        value = jnp.where(kind == 0, row0[0], jnp.where(kind == 1, pltpu.roll(row0[1], 1, 0), 0.0))
        return jnp.where(kind == 2, edge[0], jnp.where(kind == 3, edge[1], value))

    def extra_store(shard, cell, new_re, new_im):
        if not upward:
            extras[shard * cells + cell, 0] = new_re
            extras[shard * cells + cell, 1] = new_im
            return
        new_re = new_re + extras[shard * cells + cell, 0]
        new_im = new_im + extras[shard * cells + cell, 1]
        spread = [new_re, pltpu.roll(new_re, rows, 1), pltpu.roll(new_im, 2 * rows, 1), pltpu.roll(new_im, 3 * rows, 1)]
        for side in range(2):
            row = spread[0][2 + side : 3 + side]
            for group in range(1, 4):
                at_sub = 2 + side + 4 * (group % 2)
                row = jnp.where(lane < group * rows, row, spread[group][at_sub : at_sub + 1])
            outs[side].put(shard, pl.ds(plan.edge + cell, 1), row)
            for base, value in ((0, new_re), (imag_at, new_im)):
                value = pltpu.roll(value, 7, 0) if side else value
                held = outs[side].at(shard, place(cell, base, 0))
                pair = (sub % 4 == 0) & (keep[...] > 0.0)
                outs[side].put(shard, place(cell, base, 0), jnp.where(pair, 0.5 * (held + value), held))

    for count in range(2 * tiles + (1 if at == 0 else 0)):
        extra = count == 2 * tiles
        side, tile = (2, tiles) if extra else (count // tiles, count % tiles)
        inv_re = [inv[0, d, count] for d in range(6)]
        inv_im = [inv[1, d, count] for d in range(6)]
        fresh = extra or tile == 0

        def block(step, psi, extra=extra, side=side, tile=tile, inv_re=inv_re, inv_im=inv_im, fresh=fresh):
            psi_re, psi_im = list(psi[:6]), list(psi[6:])
            shard = step if upward else plan.shards - 1 - step
            for cell in range(cells) if upward else range(cells - 1, -1, -1):
                z = shard * cells + cell
                if extra:
                    row_re, row_im = extra_source(shard, cell, 0), extra_source(shard, cell, imag_at)
                else:
                    row_re = specs[side].at(shard, place(cell, 0, tile))
                    row_im = specs[side].at(shard, place(cell, imag_at, tile))
                row_re, row_im = rate[side] * row_re, rate[side] * row_im
                aim_re, aim_im = aims[z, 0, tile], aims[z, 1, tile]
                for d in range(6):
                    sum_re = row_re + couple[side, d] * psi_re[d]
                    sum_im = row_im + couple[side, d] * psi_im[d]
                    psi_re[d] = inv_re[d] * sum_re - inv_im[d] * sum_im
                    psi_im[d] = inv_re[d] * sum_im + inv_im[d] * sum_re
                    product = psi_re[d] * aim_re + psi_im[d] * aim_im
                    totals[side, d, z] = product if fresh else totals[side, d, z] + product
                new_re = ((psi_re[0] + psi_re[1]) + (psi_re[2] + psi_re[3])) + (psi_re[4] + psi_re[5])
                new_im = ((psi_im[0] + psi_im[1]) + (psi_im[2] + psi_im[3])) + (psi_im[4] + psi_im[5])
                if extra:
                    extra_store(shard, cell, new_re, new_im)
                    continue
                if upward:
                    new_re = new_re + parts[side].at(shard, place(cell, 0, tile))
                    new_im = new_im + parts[side].at(shard, place(cell, imag_at, tile))
                outs[side].put(shard, place(cell, 0, tile), new_re)
                outs[side].put(shard, place(cell, imag_at, tile), new_im)
            return tuple(psi_re + psi_im)

        if upward:
            start = []
            for part in range(2):
                value = fluxes[0][part, tile]
                for other in fluxes[1:]:
                    value = value + other[part, tile]
                start += [share[side] * value] * 6
        else:
            start = [zeros] * 12
        carried = lax.fori_loop(0, plan.shards, block, tuple(start))
        if not upward:
            for part in range(2):
                value = carried[6 * part] * cosine[0]
                for d in range(1, 6):
                    value = value + carried[6 * part + d] * cosine[d]
                value = value + pltpu.roll(value, 4, 0)
                if extra:
                    swapped = jnp.where(sub % 2 == 0, pltpu.roll(value, 7, 0), pltpu.roll(value, 1, 0))
                    flux[part, tile] = value + swapped
                elif side == 0:
                    flux[part, tile] = value
                else:
                    flux[part, tile] = flux[part, tile] + value
    for side in range(3 if at == 0 else 2):
        for d in range(6):
            sums[side, d] = jnp.sum(totals[side, d], axis=-1)


def sweep(plan, at, upward, groups, *operands):
    tiles = plan.steps(at)
    sides = 3 if at == 0 else 2
    vmem = pl.BlockSpec(memory_space=pltpu.VMEM)
    out_shape = plan.shapes(at, plan.sides_back(at) if upward else 2)
    if not upward:
        out_shape.append(jax.ShapeDtypeStruct((2, tiles, 8, LANES), jnp.float32))
    out_shape.append(jax.ShapeDtypeStruct((sides, 6, plan.depth, 8), jnp.float32))
    if not upward and at == 0:
        out_shape.append(jax.ShapeDtypeStruct((plan.depth, 2, 8, LANES), jnp.float32))
    return pl.pallas_call(
        functools.partial(sweep_kernel, plan, at, upward, groups),
        in_specs=[vmem] * len(operands),
        out_specs=[vmem] * len(out_shape),
        out_shape=out_shape,
        scratch_shapes=[pltpu.VMEM((sides, 6, plan.depth, 8, LANES), jnp.float32)],
        compiler_params=PARAMS,
        cost_estimate=cost(13),
        name="upward" if upward else "downward",
    )(*operands)


def mirror_kernel(plan, group, upper, lanes_turned, rows_turned, turned, lead):
    rows, half = plan.rows, plan.half
    cells = rows_turned.shape[0] // rows
    for part in range(2):
        sign = 1.0 if part == 0 else -1.0
        for at in range(0, upper.shape[1], cells):
            pairs = split(sign * upper[part, at : at + cells].reshape(cells * rows, half))
            value = dot(pairs[0], lanes_turned[...]) + dot(pairs[1], lanes_turned[...])
            lead[part, at : at + cells] = value.reshape(cells, rows, half)[:, 0, :]
            pairs = split(value)
            value = dot(rows_turned[...], pairs[0]) + dot(rows_turned[...], pairs[1])
            turned[part, at : at + cells] = value.reshape(cells, rows, half)


def mirror(plan, forward, groups):
    cells = 8
    rows, half = plan.rows, plan.half
    share = plan.depth // groups
    lanes_turned = np.zeros((half, half), ml_dtypes.bfloat16)
    rows_turned = np.zeros((cells * rows, cells * rows), ml_dtypes.bfloat16)
    for k in range(1, half):
        lanes_turned[half - k, k] = 1
    for c in range(cells):
        for r in range(1, rows):
            rows_turned[c * rows + r, c * rows + rows - r] = 1
    lanes_turned, rows_turned = jnp.asarray(lanes_turned), jnp.asarray(rows_turned)
    group = lax.axis_index("ba").astype(jnp.int32).reshape(1)
    spec = pltpu.PrefetchScalarGridSpec(
        num_scalar_prefetch=1,
        grid=(forward.shape[0],),
        in_specs=[
            pl.BlockSpec((None, 2, share, rows, half), lambda step, at: (step, 0, at[0], 0, 1)),
            pl.BlockSpec(lanes_turned.shape, lambda step, at: (0, 0)),
            pl.BlockSpec(rows_turned.shape, lambda step, at: (0, 0)),
        ],
        out_specs=[
            pl.BlockSpec((None, 2, share, rows, half), lambda step, at: (step, 0, 0, 0, 0)),
            pl.BlockSpec((None, 2, share, half), lambda step, at: (step, 0, 0, 0)),
        ],
    )
    return pl.pallas_call(
        functools.partial(mirror_kernel, plan),
        grid_spec=spec,
        out_shape=[
            jax.ShapeDtypeStruct((forward.shape[0], 2, share, rows, half), jnp.float32),
            jax.ShapeDtypeStruct((forward.shape[0], 2, share, half), jnp.float32),
        ],
        compiler_params=PARAMS,
        cost_estimate=cost(5),
        name="mirrored",
    )(group, forward, lanes_turned, rows_turned)


def aims_kernel(plan, at, group, own, other, keep, out, held):
    half, chunk, tiles = plan.half, plan.chunk, plan.tiles
    cells, rows = own.shape[1:3]
    row = lax.broadcasted_iota(jnp.int32, (chunk, half), 0)
    sub = lax.broadcasted_iota(jnp.int32, (8, LANES), 0)
    lane = lax.broadcasted_iota(jnp.int32, (1, LANES), 1)
    for part in range(2):
        if at == 0:
            owner = keep[...] > 0.0
            line = own[part, :, :, half:].reshape(cells * rows, half).T[:1]
            if cells * rows < LANES:
                line = jnp.concatenate([line, jnp.zeros((1, LANES - cells * rows), jnp.float32)], axis=1)
        for cell in range(cells):
            mine, theirs = own[part, cell, :chunk, :half], other[part, cell]
            if at == 0:
                held[...] = mine + jnp.where((row == 0) & owner[:1], 0.0, theirs)
            else:
                held[...] = mine + theirs
            for tile in range(tiles):
                four = held[pl.ds(tile, 4, stride=tiles), :]
                out[cell, part, tile] = jnp.concatenate([four, four], axis=0)
            if at == 0:
                partner = jnp.where(owner, theirs[:1], 0.0)
                start = cell * rows
                piece = line[:, start // LANES * LANES : start // LANES * LANES + LANES]
                at_zero = pltpu.roll(piece, LANES - start % LANES, 1) if start % LANES else piece
                out[cell, part, tiles] = jnp.where(sub % 4 < 2, partner, jnp.where(lane < rows, at_zero, 0.0))


def make_aims(plan, at, own, parts, keep, step):
    cells = 8
    half, chunk = plan.half, plan.chunk
    other = jnp.stack(parts)
    groups = other.shape[0]
    blocks = other.shape[2] // cells
    group = lax.axis_index("ba").astype(jnp.int32).reshape(1)
    own_rows = plan.rows if at == 0 else chunk

    def sender(z, me):
        return (lax.rem(me[0] + groups - z // blocks, groups), 0, z % blocks, 0, 0)

    spec = pltpu.PrefetchScalarGridSpec(
        num_scalar_prefetch=1,
        grid=(plan.depth // cells,),
        in_specs=[
            pl.BlockSpec((None, 2, cells, own_rows, plan.width), lambda z, me: (step, 0, z, at, 0)),
            pl.BlockSpec((None, 2, cells, chunk, half), sender),
            pl.BlockSpec(keep.shape, lambda z, me: (0, 0)),
        ],
        out_specs=pl.BlockSpec((cells, 2, plan.steps(at), 8, LANES), lambda z, me: (z, 0, 0, 0, 0)),
        scratch_shapes=[pltpu.VMEM((chunk, half), jnp.float32)],
    )
    return pl.pallas_call(
        functools.partial(aims_kernel, plan, at),
        grid_spec=spec,
        out_shape=jax.ShapeDtypeStruct((plan.depth, 2, plan.steps(at), 8, LANES), jnp.float32),
        compiler_params=PARAMS,
        cost_estimate=cost(4),
        name="targets",
    )(group, own, other, keep)


def lift(value):
    main = jnp.broadcast_to(value.reshape(2, 2, 1), (2, 2, 4)).reshape(2, 8)
    extra = jnp.broadcast_to(value.reshape(2, 2).T[:, None, :], (2, 2, 2)).reshape(1, 8)
    return jnp.broadcast_to(jnp.concatenate([main, extra])[:, :, None], (3, 8, LANES))


def factors(plan, at, place, rate, speed):
    unit = 1.5 * 2.0 * math.pi / plan.width
    half, width, tiles = plan.half, plan.width, plan.tiles
    base = place * plan.rows
    sub = jnp.arange(8)

    def signed(index):
        return ((index + half) % width - half).astype(jnp.float32) * unit

    row = base + at * plan.chunk + jnp.arange(tiles)[:, None] + tiles * (sub % 4)[None, :]
    freq_x = jnp.broadcast_to(signed(row)[None, :, :, None], (2, tiles, 8, LANES)).reshape(2 * tiles, 8, LANES)
    freq_y = jnp.broadcast_to(signed(jnp.arange(LANES)), (2 * tiles, 8, LANES))
    sides = [0] * tiles + [1] * tiles
    if at == 0:
        partner = (sub % 4 < 2)[:, None]
        extra_x = jnp.where(partner, -signed(base), signed(base + jnp.arange(LANES) % plan.rows)[None, :])
        extra_y = jnp.where(partner, signed(jnp.arange(LANES))[None, :], signed(jnp.asarray(half)))
        freq_x = jnp.concatenate([freq_x, extra_x[None]], axis=0)
        freq_y = jnp.concatenate([freq_y, extra_y[None]], axis=0)
        sides.append(2)
    rate, speed = [jnp.concatenate([v[s : s + 1] for s in sides]) for v in (rate, speed)]
    cosine, along_x, along_y = [np.asarray(q, np.float32).reshape(12, 1, 1, 1) for q in quadrature()]
    wave = speed * (along_x * freq_x + along_y * freq_y)
    real = rate + np.abs(cosine) * speed
    denom = real * real + wave * wave
    return jnp.stack([real / denom, -wave / denom])


def body(phi_start, coeff, forward, rates, speeds, shares):
    shards = lax.axis_size("gx")
    groups = lax.axis_size("ba")
    place = lax.axis_index("gx")
    cells, bands, width, _ = phi_start.shape
    rows = forward.shape[3]
    steps = forward.shape[0]
    plan = Plan(shards, cells, width, rows)
    depth = plan.depth
    consts = [jnp.asarray(part) for part in tables(width)]
    owner = place * rows == plan.half
    keep = jnp.broadcast_to(jnp.where(owner, 1.0, 0.0).astype(jnp.float32), (8, LANES))
    rate, speed, share = lift(rates), lift(speeds), lift(shares)
    polar = np.abs(np.asarray(quadrature()[0][:6], np.float32)).reshape(1, 6, 1, 1)
    couple = polar * speed[:, None]
    inverse = [factors(plan, at, place, rate, speed) for at in range(plan.chunks)]

    def tie(value, *others):
        return lax.optimization_barrier((value, *others))[0]

    def swap_targets(turned, lead):
        turned = lax.ppermute(turned, "gx", [(i, shards - 1 - i) for i in range(shards)])
        lead = lax.ppermute(lead, "gx", [(i, (shards - i) % shards) for i in range(shards)])
        return jnp.where(jnp.arange(rows)[:, None] == 0, lead[:, :, :, None, :], turned)

    def spread_targets(turned):
        parts = [turned]
        for shift in range(1, groups):
            parts.append(lax.ppermute(turned, "ba", [(i, (i + shift) % groups) for i in range(groups)]))
        return parts

    def exchange(array):
        return lax.all_to_all(array, "gx", split_axis=0, concat_axis=0, tiled=True)

    main_sums, extra_sums = [[], []], [[], []]

    def collect(sums, way):
        main_sums[way].append(sums[:2])
        if sums.shape[0] == 3:
            extra_sums[way].append(sums[2])

    def into(transform):
        pieces, held = [[] for _ in range(plan.chunks)], None
        for side in range(2):
            held = transform(side, held)
            for at in range(plan.chunks):
                if plan.sides_sent(at) == 2 or side == 1:
                    pieces[at].append(held[at])
        return pieces

    def in_order(pieces, after, besides=()):
        arrived = []
        for piece in pieces:
            if after is not None:
                piece = tie(piece, after, *besides)
            after = exchange(piece)
            arrived.append(after)
        return arrived

    flipped = mirror(plan, forward, groups)
    swapped = swap_targets(*flipped)
    starts = [tie(phi_start, *flipped), tie(phi_start, swapped)]
    sent = into(lambda side, held: first(plan, side, starts[side], consts, held))
    chunk_rows = [slice(at * plan.chunk, (at + 1) * plan.chunk) for at in range(plan.chunks)]
    spread = [[spread_targets(swapped[step][:, :, held]) for held in chunk_rows] for step in range(steps)]
    early = make_aims(plan, 0, forward, spread[0][0], keep, 0)
    for step in range(steps):
        modes, after = [], None
        for at in range(plan.chunks):
            besides = ()
            if step == 0:
                besides = spread[0][at]
                if at == 1:
                    besides = [*besides, early]
            modes.append(in_order(sent[at], after, besides))
            after = modes[at][-1]
        back = []
        back = []
        for at in range(plan.chunks):
            inv = inverse[at]
            aims = early if step == 0 and at == 0 else make_aims(plan, at, forward, spread[step][at], keep, step)
            common = (*modes[at], aims)
            part0, part1, flux, sums, *extras = sweep(plan, at, False, groups, *common, inv[:, :6], couple, rate)
            collect(sums, 0)
            fluxes = [flux]
            for shift in range(1, groups):
                fluxes.append(lax.ppermute(flux, "ba", [(i, (i + shift) % groups) for i in range(groups)]))
            rest = (part0, part1, *extras, share, keep, *fluxes)
            *new, sums = sweep(plan, at, True, groups, *common, inv[:, 6:], couple, rate, *rest)
            collect(sums, 1)
            if step + 1 < steps and at == plan.chunks - 1:
                for part, parts in enumerate(spread[step + 1]):
                    new[part % len(new)] = tie(new[part % len(new)], *parts)
            back.append(in_order(new, back[-1][-1] if back else None))
        ends = [[pieces[side % len(pieces)] for pieces in back] for side in range(2)]
        if step + 1 < steps:
            sent = into(lambda side, held: middle(plan, side, ends[side], coeff, consts, held))
        else:
            upper = last(plan, 0, ends[0], coeff, consts, None)
            phi = last(plan, 1, ends[1], coeff, consts, upper)

    grads = []
    for way in range(2):
        main = sum(main_sums[way]).reshape(2, 6, depth, 2, 4).sum(axis=4)
        extra = sum(extra_sums[way]).reshape(6, depth, 2, 2, 2).sum(axis=3)
        grads.append(main.transpose(2, 1, 0, 3) + extra.transpose(1, 0, 3, 2))
    sums = jnp.stack(grads, axis=1).reshape(shards, cells * 12 * bands) * (1.0 / width)
    grad = exchange(tie(sums, back[-1][-1], upper)).sum(axis=0).reshape(cells, 12, bands)
    return (phi, grad)


def solution(mesh):
    in_specs = (
        P("gx", "ba", None, None),
        P("gx", None, None),
        P(None, None, None, "gx", None),
        P("ba"),
        P("ba"),
        P("ba"),
    )
    out_specs = (P("gx", "ba", None, None), P("gx", None, "ba"))
    return jax.shard_map(body, mesh=mesh, in_specs=in_specs, out_specs=out_specs, check_vma=False)
```

```python
import functools
import math

import jax
import jax.numpy as jnp
import ml_dtypes
import numpy as np
from jax import lax
from jax.experimental import pallas as pl
from jax.experimental.pallas import tpu as pltpu
from jax.sharding import PartitionSpec as P

LANES = 128
VMEM = 56 * 1024 * 1024
CHUNK_ROWS = 16


def split_host(table):
    high = table.astype(ml_dtypes.bfloat16)
    low = (table - high.astype(np.float64)).astype(ml_dtypes.bfloat16)
    return high, low


def tables(count):
    half = count // 2
    index = np.arange(count)
    angle = (np.outer(index, index) % count) * (2.0 * np.pi / count)
    cos, sin = np.cos(angle) / math.sqrt(count), np.sin(angle) / math.sqrt(count)
    alternate = np.where(index % 2 == 0, 1.0, -1.0) / math.sqrt(count)
    into = np.concatenate([cos[:, :half], alternate[:, None], -sin[:, 1:half]], axis=1)
    weight = np.where(np.arange(half) == 0, 1.0, 2.0)[:, None]
    back = np.concatenate([weight * cos[:half], alternate[None], -2.0 * sin[1:half]], axis=0) / 12.0
    stacked = np.concatenate([cos, sin], axis=0)
    beside = np.concatenate([cos, sin], axis=1)
    return [part for table in (into, stacked, beside, back) for part in split_host(table)]


def quadrature():
    level = np.arange(6)
    polar = 0.2 + 0.15 * level
    cosine = np.concatenate([-polar, polar])
    azimuth = np.concatenate([level * (np.pi / 3.0) + np.pi / 6.0, level * (np.pi / 3.0)])
    sine = np.sqrt(1.0 - cosine * cosine)
    return (cosine, sine * np.cos(azimuth), sine * np.sin(azimuth))


def split(value):
    high = value.astype(jnp.bfloat16)
    low = (value - high.astype(jnp.float32)).astype(jnp.bfloat16)
    return high, low


def dot(left, right):
    return jnp.dot(left, right, preferred_element_type=jnp.float32)


def dot3(left, right):
    return dot(left[0], right[0]) + (dot(left[0], right[1]) + dot(left[1], right[0]))


class Plan:
    def __init__(self, shards, cells, width, rows):
        self.shards, self.cells, self.width, self.rows = shards, cells, width, rows
        self.half = width // 2
        self.chunk = min(CHUNK_ROWS, rows)
        self.chunks = rows // self.chunk
        self.tiles = self.chunk // 4
        self.main = 4 * self.chunk
        self.depth = shards * cells
        self.edge = cells * self.main
        self.batch = 2 if cells % 2 == 0 else 1
        self.pad = (cells + 7) // 8 * 8

    def height(self, chunk):
        return self.edge + (self.pad if chunk == 0 else 0)

    def shapes(self, chunk, sides):
        return [jax.ShapeDtypeStruct((self.shards, 2 // sides * self.height(chunk), LANES), jnp.float32)] * sides

    def sides_sent(self, chunk):
        return 2 if chunk == 0 else 1

    def sides_back(self, chunk):
        return 2 if chunk == self.chunks - 1 else 1

    def steps(self, chunk):
        return self.tiles + (1 if chunk == 0 else 0)


class View:
    def __init__(self, ref, offset=0):
        self.ref, self.offset = ref, offset

    def moved(self, rows):
        return pl.ds(self.offset + rows.start, rows.size, stride=rows.stride)

    def at(self, shard, rows):
        return self.ref[shard, self.moved(rows), :]

    def put(self, shard, rows, value):
        self.ref[shard, self.moved(rows), :] = value


def views(plan, at, refs):
    if len(refs) == 2:
        return [View(ref) for ref in refs]
    return [View(refs[0], side * plan.height(at)) for side in range(2)]


def forward_slabs(plan, step, phis, into, stacked, outs):
    for sub in range(plan.batch):
        forward_cell(plan, step * plan.batch + sub, sub, functools.partial(phis, sub), into, stacked, outs)


def forward_cell(plan, cell, sub, phis, into, stacked, outs):
    width, half, rows, chunk = plan.width, plan.half, plan.rows, plan.chunk
    lane = lax.broadcasted_iota(jnp.int32, (width, half), 1)
    first = lane == 0
    columns = jnp.zeros((width, half), jnp.float32)
    for band in range(2):
        packed = dot3(split(phis(band)), into)
        both = dot3(stacked, split(packed))
        cos_re, cos_im = both[:width, :half], both[:width, half:]
        sin_re, sin_im = both[width:, :half], both[width:, half:]
        real = cos_re + jnp.where(first, 0.0, sin_im)
        imag = jnp.where(first, 0.0, cos_im) - sin_re
        for at in range(plan.chunks):
            base = pl.multiple_of(cell * plan.main, 8) if at == 0 else sub * plan.main
            for shard in range(plan.shards):
                start = shard * rows + at * chunk
                outs[at][shard, pl.ds(base + band * chunk, chunk), :] = real[start : start + chunk]
                outs[at][shard, pl.ds(base + (2 + band) * chunk, chunk), :] = imag[start : start + chunk]
        columns = jnp.where(lane == band, pltpu.roll(cos_im, band, 1) if band else cos_im, columns)
        columns = jnp.where(lane == band + 2, -pltpu.roll(sin_im, band + 2, 1), columns)
    turned = columns.T[:8]
    slot = lax.broadcasted_iota(jnp.int32, (1, LANES), 1)
    for shard in range(plan.shards):
        start = shard * rows
        piece = turned[:, start // LANES * LANES : start // LANES * LANES + LANES]
        row = jnp.zeros((1, LANES), jnp.float32)
        for group in range(4):
            shift = (group * rows - start) % LANES
            held = pltpu.roll(piece, shift, 1) if shift else piece
            row = jnp.where((slot >= group * rows) & (slot < (group + 1) * rows), held[group : group + 1], row)
        outs[0][shard, pl.ds(plan.edge + cell, 1), :] = row


def inverse_slabs(plan, step, ins, beside, back, take):
    width = plan.width
    uppers, lowers = [], []
    for sub in range(plan.batch):
        inverse_cell(plan, step * plan.batch + sub, sub, ins, uppers, lowers)
    pairs = jnp.concatenate([jnp.concatenate(uppers, axis=1), jnp.concatenate(lowers, axis=1)], axis=0)
    mixed = dot3(beside, split(pairs))
    slabs = [mixed[:, i * width : (i + 1) * width] for i in range(2 * plan.batch)]
    out = dot3(split(jnp.concatenate(slabs, axis=0)), back)
    for sub in range(plan.batch):
        for band in range(2):
            start = (2 * sub + band) * width
            take(sub, band, out[start : start + width])


def inverse_cell(plan, cell, sub, ins, uppers, lowers):
    width, half, rows, chunk = plan.width, plan.half, plan.rows, plan.chunk
    lines = [ins[0][shard, pl.ds(plan.edge + cell, 1), :] for shard in range(plan.shards)]
    lines.append(jnp.zeros((LANES - plan.shards, LANES), jnp.float32))
    turned = jnp.concatenate(lines, axis=0).T[: 4 * rows]
    shifted = [pltpu.roll(turned, LANES - shard, 1) if shard else turned for shard in range(plan.shards)]
    sides = [jnp.concatenate([held[g * rows : (g + 1) * rows] for held in shifted], axis=0) for g in range(4)]
    first = lax.broadcasted_iota(jnp.int32, (width, half), 1) == 0
    for band in range(2):
        reals, imags = [], []
        for shard in range(plan.shards):
            for at in range(plan.chunks):
                base = pl.multiple_of(cell * plan.main, 8) if at == 0 else sub * plan.main
                reals.append(ins[at][shard, pl.ds(base + band * chunk, chunk), :])
                imags.append(ins[at][shard, pl.ds(base + (2 + band) * chunk, chunk), :])
        real, imag = jnp.concatenate(reals, axis=0), jnp.concatenate(imags, axis=0)
        uppers += [real, jnp.where(first, sides[band], imag)]
        lowers += [-imag, jnp.where(first, -sides[band + 2], real)]


def first_kernel(plan, kept, phi, into_h, into_l, stacked_h, stacked_l, *refs):
    cell = pl.program_id(0)
    outs = refs[kept:]
    into, stacked = (into_h[...], into_l[...]), (stacked_h[...], stacked_l[...])
    forward_slabs(plan, cell, lambda sub, band: phi[sub, band], into, stacked, outs)


def middle_kernel(plan, kept, *refs):
    cell = pl.program_id(0)
    ins = refs[: plan.chunks]
    coeff = refs[plan.chunks]
    into_h, into_l, stacked_h, stacked_l, beside_h, beside_l, back_h, back_l = refs[plan.chunks + 1 : plan.chunks + 9]
    outs, held = refs[plan.chunks + 9 + kept : -1], refs[-1]

    def take(sub, band, value):
        held[sub, band] = value * coeff[sub]

    inverse_slabs(plan, cell, ins, (beside_h[...], beside_l[...]), (back_h[...], back_l[...]), take)
    into, stacked = (into_h[...], into_l[...]), (stacked_h[...], stacked_l[...])
    forward_slabs(plan, cell, lambda sub, band: held[sub, band], into, stacked, outs)


def last_kernel(plan, *refs):
    ins = refs[: plan.chunks]
    coeff, beside_h, beside_l, back_h, back_l = refs[plan.chunks : plan.chunks + 5]
    out = refs[-1]

    def take(sub, band, value):
        out[sub, band] = value * coeff[sub]

    inverse_slabs(plan, pl.program_id(0), ins, (beside_h[...], beside_l[...]), (back_h[...], back_l[...]), take)


def whole(array):
    rank = len(array.shape)
    return pl.BlockSpec(array.shape, lambda cell: (0,) * rank)


def piece_specs(plan, side, sides):
    specs = []
    for at in range(plan.chunks):
        merged = sides(at) == 1
        if at == 0:
            shape = (plan.shards, plan.height(0), LANES)
            specs.append(pl.BlockSpec(shape, lambda cell, first=side if merged else 0: (0, first, 0)))
        else:
            shape = (plan.shards, plan.batch * plan.main, LANES)
            first = side * plan.cells // plan.batch if merged else 0
            specs.append(pl.BlockSpec(shape, lambda cell, first=first: (0, first + cell, 0)))
    return specs


def sent_shapes(plan):
    return [plan.shapes(at, plan.sides_sent(at))[0] for at in range(plan.chunks)]


def slab_spec(plan, side):
    return pl.BlockSpec((plan.batch, 2, plan.width, plan.width), lambda cell: (cell, side, 0, 0))


def coeff_spec(plan):
    return pl.BlockSpec((plan.batch, plan.width, plan.width), lambda cell: (cell, 0, 0))


def cost(microseconds):
    return pl.CostEstimate(flops=0, bytes_accessed=int(microseconds * 3.69e6), transcendentals=0)


PARAMS = pltpu.CompilerParams(vmem_limit_bytes=VMEM)


def send(kernel, plan, side, operands, in_specs, held, microseconds, scratch, name):
    aliases = {}
    for at in range(plan.chunks):
        if held is not None and plan.sides_sent(at) == 1:
            aliases[len(operands)] = at
            operands, in_specs = operands + [held[at]], in_specs + [pl.BlockSpec(memory_space=pl.ANY)]
    return pl.pallas_call(
        functools.partial(kernel, plan, len(aliases)),
        grid=(plan.cells // plan.batch,),
        in_specs=in_specs,
        out_specs=piece_specs(plan, side, plan.sides_sent),
        out_shape=sent_shapes(plan),
        input_output_aliases=aliases,
        scratch_shapes=scratch,
        compiler_params=PARAMS,
        cost_estimate=cost(microseconds),
        name=name,
    )(*operands)


def first(plan, side, phi, consts, held):
    in_specs = [slab_spec(plan, side)] + [whole(c) for c in consts[:4]]
    return send(first_kernel, plan, side, [phi, *consts[:4]], in_specs, held, 12, [], "into_modes")


def middle(plan, side, ins, coeff, consts, held):
    in_specs = piece_specs(plan, side, plan.sides_back) + [coeff_spec(plan)] + [whole(c) for c in consts]
    scratch = [pltpu.VMEM((plan.batch, 2, plan.width, plan.width), jnp.float32)]
    return send(middle_kernel, plan, side, [*ins, coeff, *consts], in_specs, held, 25, scratch, "between_steps")


def last(plan, side, ins, coeff, consts, held):
    operands = [*ins, coeff, *consts[4:]]
    in_specs = piece_specs(plan, side, plan.sides_back) + [coeff_spec(plan)] + [whole(c) for c in consts[4:]]
    aliases = {}
    if held is not None:
        aliases = {len(operands): 0}
        operands.append(held)
        in_specs.append(pl.BlockSpec(memory_space=pl.ANY))
    return pl.pallas_call(
        functools.partial(last_kernel, plan),
        grid=(plan.cells // plan.batch,),
        in_specs=in_specs,
        out_specs=slab_spec(plan, side),
        out_shape=jax.ShapeDtypeStruct((plan.cells, 4, plan.width, plan.width), jnp.float32),
        input_output_aliases=aliases,
        compiler_params=PARAMS,
        cost_estimate=cost(16),
        name="out_of_modes",
    )(*operands)


def sweep_kernel(plan, at, upward, groups, *refs):
    refs = list(refs)

    def pop(count):
        taken = refs[:count]
        del refs[:count]
        return taken

    specs = views(plan, at, pop(plan.sides_sent(at)))
    aims, inv, couple, rate = pop(4)
    if upward:
        parts = views(plan, at, pop(2))
        extras = pop(1)[0] if at == 0 else None
        share, keep = pop(2)
        fluxes = pop(groups)
        outs = views(plan, at, pop(plan.sides_back(at)))
        sums, totals = refs
    else:
        outs = views(plan, at, pop(2))
        flux, sums = pop(2)
        extras = pop(1)[0] if at == 0 else None
        totals = refs[0]
    tiles, depth, cells, main, rows = plan.tiles, plan.depth, plan.cells, plan.main, plan.rows
    imag_at = 2 * plan.chunk
    sub = lax.broadcasted_iota(jnp.int32, (8, LANES), 0)
    lane = lax.broadcasted_iota(jnp.int32, (1, LANES), 1)
    zeros = jnp.zeros((8, LANES), jnp.float32)
    cosine = [abs(float(c)) / 12.0 for c in quadrature()[0][:6]]

    def place(cell, base, tile):
        return pl.ds(cell * main + base + tile, 8, stride=tiles)

    def extra_source(shard, cell, base):
        edge = []
        for s in range(2):
            line = specs[s].at(shard, pl.ds(plan.edge + cell, 1))
            line = pltpu.roll(line, LANES - 2 * rows, 1) if base else line
            edge.append(jnp.where(sub < 4, line, pltpu.roll(line, LANES - rows, 1)))
        row0 = [specs[s].at(shard, place(cell, base, 0)) for s in range(2)]
        kind = sub % 4
        value = jnp.where(kind == 0, row0[0], jnp.where(kind == 1, pltpu.roll(row0[1], 1, 0), 0.0))
        return jnp.where(kind == 2, edge[0], jnp.where(kind == 3, edge[1], value))

    def extra_store(shard, cell, new_re, new_im):
        if not upward:
            extras[shard * cells + cell, 0] = new_re
            extras[shard * cells + cell, 1] = new_im
            return
        new_re = new_re + extras[shard * cells + cell, 0]
        new_im = new_im + extras[shard * cells + cell, 1]
        spread = [new_re, pltpu.roll(new_re, rows, 1), pltpu.roll(new_im, 2 * rows, 1), pltpu.roll(new_im, 3 * rows, 1)]
        for side in range(2):
            row = spread[0][2 + side : 3 + side]
            for group in range(1, 4):
                at_sub = 2 + side + 4 * (group % 2)
                row = jnp.where(lane < group * rows, row, spread[group][at_sub : at_sub + 1])
            outs[side].put(shard, pl.ds(plan.edge + cell, 1), row)
            for base, value in ((0, new_re), (imag_at, new_im)):
                value = pltpu.roll(value, 7, 0) if side else value
                held = outs[side].at(shard, place(cell, base, 0))
                pair = (sub % 4 == 0) & (keep[...] > 0.0)
                outs[side].put(shard, place(cell, base, 0), jnp.where(pair, 0.5 * (held + value), held))

    for count in range(2 * tiles + (1 if at == 0 else 0)):
        extra = count == 2 * tiles
        side, tile = (2, tiles) if extra else (count // tiles, count % tiles)
        inv_re = [inv[0, d, count] for d in range(6)]
        inv_im = [inv[1, d, count] for d in range(6)]
        fresh = extra or tile == 0

        def block(step, psi, extra=extra, side=side, tile=tile, inv_re=inv_re, inv_im=inv_im, fresh=fresh):
            psi_re, psi_im = list(psi[:6]), list(psi[6:])
            shard = step if upward else plan.shards - 1 - step
            for cell in range(cells) if upward else range(cells - 1, -1, -1):
                z = shard * cells + cell
                if extra:
                    row_re, row_im = extra_source(shard, cell, 0), extra_source(shard, cell, imag_at)
                else:
                    row_re = specs[side].at(shard, place(cell, 0, tile))
                    row_im = specs[side].at(shard, place(cell, imag_at, tile))
                row_re, row_im = rate[side] * row_re, rate[side] * row_im
                aim_re, aim_im = aims[z, 0, tile], aims[z, 1, tile]
                for d in range(6):
                    sum_re = row_re + couple[side, d] * psi_re[d]
                    sum_im = row_im + couple[side, d] * psi_im[d]
                    psi_re[d] = inv_re[d] * sum_re - inv_im[d] * sum_im
                    psi_im[d] = inv_re[d] * sum_im + inv_im[d] * sum_re
                    product = psi_re[d] * aim_re + psi_im[d] * aim_im
                    totals[side, d, z] = product if fresh else totals[side, d, z] + product
                new_re = ((psi_re[0] + psi_re[1]) + (psi_re[2] + psi_re[3])) + (psi_re[4] + psi_re[5])
                new_im = ((psi_im[0] + psi_im[1]) + (psi_im[2] + psi_im[3])) + (psi_im[4] + psi_im[5])
                if extra:
                    extra_store(shard, cell, new_re, new_im)
                    continue
                if upward:
                    new_re = new_re + parts[side].at(shard, place(cell, 0, tile))
                    new_im = new_im + parts[side].at(shard, place(cell, imag_at, tile))
                outs[side].put(shard, place(cell, 0, tile), new_re)
                outs[side].put(shard, place(cell, imag_at, tile), new_im)
            return tuple(psi_re + psi_im)

        if upward:
            start = []
            for part in range(2):
                value = fluxes[0][part, tile]
                for other in fluxes[1:]:
                    value = value + other[part, tile]
                start += [share[side] * value] * 6
        else:
            start = [zeros] * 12
        carried = lax.fori_loop(0, plan.shards, block, tuple(start))
        if not upward:
            for part in range(2):
                value = carried[6 * part] * cosine[0]
                for d in range(1, 6):
                    value = value + carried[6 * part + d] * cosine[d]
                value = value + pltpu.roll(value, 4, 0)
                if extra:
                    swapped = jnp.where(sub % 2 == 0, pltpu.roll(value, 7, 0), pltpu.roll(value, 1, 0))
                    flux[part, tile] = value + swapped
                elif side == 0:
                    flux[part, tile] = value
                else:
                    flux[part, tile] = flux[part, tile] + value
    for side in range(3 if at == 0 else 2):
        for d in range(6):
            sums[side, d] = jnp.sum(totals[side, d], axis=-1)


def sweep(plan, at, upward, groups, *operands):
    tiles = plan.steps(at)
    sides = 3 if at == 0 else 2
    vmem = pl.BlockSpec(memory_space=pltpu.VMEM)
    out_shape = plan.shapes(at, plan.sides_back(at) if upward else 2)
    if not upward:
        out_shape.append(jax.ShapeDtypeStruct((2, tiles, 8, LANES), jnp.float32))
    out_shape.append(jax.ShapeDtypeStruct((sides, 6, plan.depth, 8), jnp.float32))
    if not upward and at == 0:
        out_shape.append(jax.ShapeDtypeStruct((plan.depth, 2, 8, LANES), jnp.float32))
    return pl.pallas_call(
        functools.partial(sweep_kernel, plan, at, upward, groups),
        in_specs=[vmem] * len(operands),
        out_specs=[vmem] * len(out_shape),
        out_shape=out_shape,
        scratch_shapes=[pltpu.VMEM((sides, 6, plan.depth, 8, LANES), jnp.float32)],
        compiler_params=PARAMS,
        cost_estimate=cost(13),
        name="upward" if upward else "downward",
    )(*operands)


def mirror_kernel(plan, group, upper, lanes_turned, rows_turned, turned, lead):
    rows, half = plan.rows, plan.half
    cells = rows_turned.shape[0] // rows
    for part in range(2):
        sign = 1.0 if part == 0 else -1.0
        for at in range(0, upper.shape[1], cells):
            pairs = split(sign * upper[part, at : at + cells].reshape(cells * rows, half))
            value = dot(pairs[0], lanes_turned[...]) + dot(pairs[1], lanes_turned[...])
            lead[part, at : at + cells] = value.reshape(cells, rows, half)[:, 0, :]
            pairs = split(value)
            value = dot(rows_turned[...], pairs[0]) + dot(rows_turned[...], pairs[1])
            turned[part, at : at + cells] = value.reshape(cells, rows, half)


def mirror(plan, forward, groups):
    cells = 8
    rows, half = plan.rows, plan.half
    share = plan.depth // groups
    lanes_turned = np.zeros((half, half), ml_dtypes.bfloat16)
    rows_turned = np.zeros((cells * rows, cells * rows), ml_dtypes.bfloat16)
    for k in range(1, half):
        lanes_turned[half - k, k] = 1
    for c in range(cells):
        for r in range(1, rows):
            rows_turned[c * rows + r, c * rows + rows - r] = 1
    lanes_turned, rows_turned = jnp.asarray(lanes_turned), jnp.asarray(rows_turned)
    group = lax.axis_index("ba").astype(jnp.int32).reshape(1)
    spec = pltpu.PrefetchScalarGridSpec(
        num_scalar_prefetch=1,
        grid=(forward.shape[0],),
        in_specs=[
            pl.BlockSpec((None, 2, share, rows, half), lambda step, at: (step, 0, at[0], 0, 1)),
            pl.BlockSpec(lanes_turned.shape, lambda step, at: (0, 0)),
            pl.BlockSpec(rows_turned.shape, lambda step, at: (0, 0)),
        ],
        out_specs=[
            pl.BlockSpec((None, 2, share, rows, half), lambda step, at: (step, 0, 0, 0, 0)),
            pl.BlockSpec((None, 2, share, half), lambda step, at: (step, 0, 0, 0)),
        ],
    )
    return pl.pallas_call(
        functools.partial(mirror_kernel, plan),
        grid_spec=spec,
        out_shape=[
            jax.ShapeDtypeStruct((forward.shape[0], 2, share, rows, half), jnp.float32),
            jax.ShapeDtypeStruct((forward.shape[0], 2, share, half), jnp.float32),
        ],
        compiler_params=PARAMS,
        cost_estimate=cost(5),
        name="mirrored",
    )(group, forward, lanes_turned, rows_turned)


def aims_kernel(plan, at, group, own, other, keep, out, held):
    half, chunk, tiles = plan.half, plan.chunk, plan.tiles
    cells, rows = own.shape[1:3]
    row = lax.broadcasted_iota(jnp.int32, (chunk, half), 0)
    sub = lax.broadcasted_iota(jnp.int32, (8, LANES), 0)
    lane = lax.broadcasted_iota(jnp.int32, (1, LANES), 1)
    for part in range(2):
        if at == 0:
            owner = keep[...] > 0.0
            line = own[part, :, :, half:].reshape(cells * rows, half).T[:1]
            if cells * rows < LANES:
                line = jnp.concatenate([line, jnp.zeros((1, LANES - cells * rows), jnp.float32)], axis=1)
        for cell in range(cells):
            mine, theirs = own[part, cell, :chunk, :half], other[part, cell]
            if at == 0:
                held[...] = mine + jnp.where((row == 0) & owner[:1], 0.0, theirs)
            else:
                held[...] = mine + theirs
            for tile in range(tiles):
                four = held[pl.ds(tile, 4, stride=tiles), :]
                out[cell, part, tile] = jnp.concatenate([four, four], axis=0)
            if at == 0:
                partner = jnp.where(owner, theirs[:1], 0.0)
                start = cell * rows
                piece = line[:, start // LANES * LANES : start // LANES * LANES + LANES]
                at_zero = pltpu.roll(piece, LANES - start % LANES, 1) if start % LANES else piece
                out[cell, part, tiles] = jnp.where(sub % 4 < 2, partner, jnp.where(lane < rows, at_zero, 0.0))


def make_aims(plan, at, own, parts, keep, step):
    cells = 8
    half, chunk = plan.half, plan.chunk
    other = jnp.stack(parts)
    groups = other.shape[0]
    blocks = other.shape[2] // cells
    group = lax.axis_index("ba").astype(jnp.int32).reshape(1)
    own_rows = plan.rows if at == 0 else chunk

    def sender(z, me):
        return (lax.rem(me[0] + groups - z // blocks, groups), 0, z % blocks, 0, 0)

    spec = pltpu.PrefetchScalarGridSpec(
        num_scalar_prefetch=1,
        grid=(plan.depth // cells,),
        in_specs=[
            pl.BlockSpec((None, 2, cells, own_rows, plan.width), lambda z, me: (step, 0, z, at, 0)),
            pl.BlockSpec((None, 2, cells, chunk, half), sender),
            pl.BlockSpec(keep.shape, lambda z, me: (0, 0)),
        ],
        out_specs=pl.BlockSpec((cells, 2, plan.steps(at), 8, LANES), lambda z, me: (z, 0, 0, 0, 0)),
        scratch_shapes=[pltpu.VMEM((chunk, half), jnp.float32)],
    )
    return pl.pallas_call(
        functools.partial(aims_kernel, plan, at),
        grid_spec=spec,
        out_shape=jax.ShapeDtypeStruct((plan.depth, 2, plan.steps(at), 8, LANES), jnp.float32),
        compiler_params=PARAMS,
        cost_estimate=cost(4),
        name="targets",
    )(group, own, other, keep)


def lift(value):
    main = jnp.broadcast_to(value.reshape(2, 2, 1), (2, 2, 4)).reshape(2, 8)
    extra = jnp.broadcast_to(value.reshape(2, 2).T[:, None, :], (2, 2, 2)).reshape(1, 8)
    return jnp.broadcast_to(jnp.concatenate([main, extra])[:, :, None], (3, 8, LANES))


def factors(plan, at, place, rate, speed):
    unit = 1.5 * 2.0 * math.pi / plan.width
    half, width, tiles = plan.half, plan.width, plan.tiles
    base = place * plan.rows
    sub = jnp.arange(8)

    def signed(index):
        return ((index + half) % width - half).astype(jnp.float32) * unit

    row = base + at * plan.chunk + jnp.arange(tiles)[:, None] + tiles * (sub % 4)[None, :]
    freq_x = jnp.broadcast_to(signed(row)[None, :, :, None], (2, tiles, 8, LANES)).reshape(2 * tiles, 8, LANES)
    freq_y = jnp.broadcast_to(signed(jnp.arange(LANES)), (2 * tiles, 8, LANES))
    sides = [0] * tiles + [1] * tiles
    if at == 0:
        partner = (sub % 4 < 2)[:, None]
        extra_x = jnp.where(partner, -signed(base), signed(base + jnp.arange(LANES) % plan.rows)[None, :])
        extra_y = jnp.where(partner, signed(jnp.arange(LANES))[None, :], signed(jnp.asarray(half)))
        freq_x = jnp.concatenate([freq_x, extra_x[None]], axis=0)
        freq_y = jnp.concatenate([freq_y, extra_y[None]], axis=0)
        sides.append(2)
    rate, speed = [jnp.concatenate([v[s : s + 1] for s in sides]) for v in (rate, speed)]
    cosine, along_x, along_y = [np.asarray(q, np.float32).reshape(12, 1, 1, 1) for q in quadrature()]
    wave = speed * (along_x * freq_x + along_y * freq_y)
    real = rate + np.abs(cosine) * speed
    denom = real * real + wave * wave
    return jnp.stack([real / denom, -wave / denom])


def body(phi_start, coeff, forward, rates, speeds, shares):
    shards = lax.axis_size("gx")
    groups = lax.axis_size("ba")
    place = lax.axis_index("gx")
    cells, bands, width, _ = phi_start.shape
    rows = forward.shape[3]
    steps = forward.shape[0]
    plan = Plan(shards, cells, width, rows)
    depth = plan.depth
    consts = [jnp.asarray(part) for part in tables(width)]
    owner = place * rows == plan.half
    keep = jnp.broadcast_to(jnp.where(owner, 1.0, 0.0).astype(jnp.float32), (8, LANES))
    rate, speed, share = lift(rates), lift(speeds), lift(shares)
    polar = np.abs(np.asarray(quadrature()[0][:6], np.float32)).reshape(1, 6, 1, 1)
    couple = polar * speed[:, None]
    inverse = [factors(plan, at, place, rate, speed) for at in range(plan.chunks)]

    def tie(value, *others):
        return lax.optimization_barrier((value, *others))[0]

    def swap_targets(turned, lead):
        turned = lax.ppermute(turned, "gx", [(i, shards - 1 - i) for i in range(shards)])
        lead = lax.ppermute(lead, "gx", [(i, (shards - i) % shards) for i in range(shards)])
        return jnp.where(jnp.arange(rows)[:, None] == 0, lead[:, :, :, None, :], turned)

    def spread_targets(turned):
        parts = [turned]
        for shift in range(1, groups):
            parts.append(lax.ppermute(turned, "ba", [(i, (i + shift) % groups) for i in range(groups)]))
        return parts

    def exchange(array):
        return lax.all_to_all(array, "gx", split_axis=0, concat_axis=0, tiled=True)

    main_sums, extra_sums = [[], []], [[], []]

    def collect(sums, way):
        main_sums[way].append(sums[:2])
        if sums.shape[0] == 3:
            extra_sums[way].append(sums[2])

    def into(transform):
        pieces, held = [[] for _ in range(plan.chunks)], None
        for side in range(2):
            held = transform(side, held)
            for at in range(plan.chunks):
                if plan.sides_sent(at) == 2 or side == 1:
                    pieces[at].append(held[at])
        return pieces

    def in_order(pieces, after, besides=()):
        arrived = []
        for piece in pieces:
            if after is not None:
                piece = tie(piece, after, *besides)
            after = exchange(piece)
            arrived.append(after)
        return arrived

    flipped = mirror(plan, forward, groups)
    swapped = swap_targets(*flipped)
    starts = [tie(phi_start, *flipped), tie(phi_start, swapped)]
    sent = into(lambda side, held: first(plan, side, starts[side], consts, held))
    chunk_rows = [slice(at * plan.chunk, (at + 1) * plan.chunk) for at in range(plan.chunks)]
    spread = [[spread_targets(swapped[step][:, :, held]) for held in chunk_rows] for step in range(steps)]
    early = make_aims(plan, 0, forward, spread[0][0], keep, 0)
    for step in range(steps):
        modes, after = [], None
        for at in range(plan.chunks):
            besides = ()
            if step == 0:
                besides = spread[0][at]
                if at == 1:
                    besides = [*besides, early]
            modes.append(in_order(sent[at], after, besides))
            after = modes[at][-1]
        back = []
        back = []
        for at in range(plan.chunks):
            inv = inverse[at]
            aims = early if step == 0 and at == 0 else make_aims(plan, at, forward, spread[step][at], keep, step)
            common = (*modes[at], aims)
            part0, part1, flux, sums, *extras = sweep(plan, at, False, groups, *common, inv[:, :6], couple, rate)
            collect(sums, 0)
            fluxes = [flux]
            for shift in range(1, groups):
                fluxes.append(lax.ppermute(flux, "ba", [(i, (i + shift) % groups) for i in range(groups)]))
            rest = (part0, part1, *extras, share, keep, *fluxes)
            *new, sums = sweep(plan, at, True, groups, *common, inv[:, 6:], couple, rate, *rest)
            collect(sums, 1)
            if step + 1 < steps and at == plan.chunks - 1:
                for part, parts in enumerate(spread[step + 1]):
                    new[part % len(new)] = tie(new[part % len(new)], *parts)
            back.append(in_order(new, back[-1][-1] if back else None))
        ends = [[pieces[side % len(pieces)] for pieces in back] for side in range(2)]
        if step + 1 < steps:
            sent = into(lambda side, held: middle(plan, side, ends[side], coeff, consts, held))
        else:
            upper = last(plan, 0, ends[0], coeff, consts, None)
            phi = last(plan, 1, ends[1], coeff, consts, upper)

    grads = []
    for way in range(2):
        main = sum(main_sums[way]).reshape(2, 6, depth, 2, 4).sum(axis=4)
        extra = sum(extra_sums[way]).reshape(6, depth, 2, 2, 2).sum(axis=3)
        grads.append(main.transpose(2, 1, 0, 3) + extra.transpose(1, 0, 3, 2))
    sums = jnp.stack(grads, axis=1).reshape(shards, cells * 12 * bands) * (1.0 / width)
    grad = exchange(tie(sums, back[-1][-1], upper)).sum(axis=0).reshape(cells, 12, bands)
    return (phi, grad)


def solution(mesh):
    in_specs = (
        P("gx", "ba", None, None),
        P("gx", None, None),
        P(None, None, None, "gx", None),
        P("ba"),
        P("ba"),
        P("ba"),
    )
    out_specs = (P("gx", "ba", None, None), P("gx", None, "ba"))
    return jax.shard_map(body, mesh=mesh, in_specs=in_specs, out_specs=out_specs, check_vma=False)
```

```python
import functools
import math

import jax
import jax.numpy as jnp
import ml_dtypes
import numpy as np
from jax import lax
from jax.experimental import pallas as pl
from jax.experimental.pallas import tpu as pltpu
from jax.sharding import PartitionSpec as P

LANES = 128
VMEM = 56 * 1024 * 1024
CHUNK_ROWS = 16


def split_host(table):
    high = table.astype(ml_dtypes.bfloat16)
    low = (table - high.astype(np.float64)).astype(ml_dtypes.bfloat16)
    return high, low


def tables(count):
    half = count // 2
    index = np.arange(count)
    angle = (np.outer(index, index) % count) * (2.0 * np.pi / count)
    cos, sin = np.cos(angle) / math.sqrt(count), np.sin(angle) / math.sqrt(count)
    alternate = np.where(index % 2 == 0, 1.0, -1.0) / math.sqrt(count)
    into = np.concatenate([cos[:, :half], alternate[:, None], -sin[:, 1:half]], axis=1)
    weight = np.where(np.arange(half) == 0, 1.0, 2.0)[:, None]
    back = np.concatenate([weight * cos[:half], alternate[None], -2.0 * sin[1:half]], axis=0) / 12.0
    stacked = np.concatenate([cos, sin], axis=0)
    beside = np.concatenate([cos, sin], axis=1)
    return [part for table in (into, stacked, beside, back) for part in split_host(table)]


def quadrature():
    level = np.arange(6)
    polar = 0.2 + 0.15 * level
    cosine = np.concatenate([-polar, polar])
    azimuth = np.concatenate([level * (np.pi / 3.0) + np.pi / 6.0, level * (np.pi / 3.0)])
    sine = np.sqrt(1.0 - cosine * cosine)
    return (cosine, sine * np.cos(azimuth), sine * np.sin(azimuth))


def split(value):
    high = value.astype(jnp.bfloat16)
    low = (value - high.astype(jnp.float32)).astype(jnp.bfloat16)
    return high, low


def dot(left, right):
    return jnp.dot(left, right, preferred_element_type=jnp.float32)


def dot3(left, right):
    return dot(left[0], right[0]) + (dot(left[0], right[1]) + dot(left[1], right[0]))


class Plan:
    def __init__(self, shards, cells, width, rows, batch=1):
        self.shards, self.cells, self.width, self.rows = shards, cells, width, rows
        self.half = width // 2
        self.chunk = min(CHUNK_ROWS, rows)
        self.chunks = rows // self.chunk
        self.tiles = self.chunk // 4
        self.main = 4 * self.chunk
        self.depth = shards * cells
        self.edge = cells * self.main
        self.batch = batch
        self.pad = (cells + 7) // 8 * 8

    def height(self, chunk):
        return self.edge + (self.pad if chunk == 0 else 0)

    def shapes(self, chunk, sides):
        return [jax.ShapeDtypeStruct((self.shards, 2 // sides * self.height(chunk), LANES), jnp.float32)] * sides

    def sides_sent(self, chunk):
        return 2 if chunk == 0 else 1

    def sides_back(self, chunk):
        return 2 if chunk == self.chunks - 1 else 1

    def steps(self, chunk):
        return self.tiles + (1 if chunk == 0 else 0)


class View:
    def __init__(self, ref, offset=0):
        self.ref, self.offset = ref, offset

    def moved(self, rows):
        return pl.ds(self.offset + rows.start, rows.size, stride=rows.stride)

    def at(self, shard, rows):
        return self.ref[shard, self.moved(rows), :]

    def put(self, shard, rows, value):
        self.ref[shard, self.moved(rows), :] = value


def views(plan, at, refs):
    if len(refs) == 2:
        return [View(ref) for ref in refs]
    return [View(refs[0], side * plan.height(at)) for side in range(2)]


def forward_slabs(plan, step, phis, into, stacked, outs):
    for sub in range(plan.batch):
        forward_cell(plan, step * plan.batch + sub, sub, functools.partial(phis, sub), into, stacked, outs)


def forward_cell(plan, cell, sub, phis, into, stacked, outs):
    width, half, rows, chunk = plan.width, plan.half, plan.rows, plan.chunk
    lane = lax.broadcasted_iota(jnp.int32, (width, half), 1)
    first = lane == 0
    columns = jnp.zeros((width, half), jnp.float32)
    for band in range(2):
        packed = dot3(split(phis(band)), into)
        both = dot3(stacked, split(packed))
        cos_re, cos_im = both[:width, :half], both[:width, half:]
        sin_re, sin_im = both[width:, :half], both[width:, half:]
        real = cos_re + jnp.where(first, 0.0, sin_im)
        imag = jnp.where(first, 0.0, cos_im) - sin_re
        for at in range(plan.chunks):
            base = pl.multiple_of(cell * plan.main, 8) if at == 0 else sub * plan.main
            for shard in range(plan.shards):
                start = shard * rows + at * chunk
                outs[at][shard, pl.ds(base + band * chunk, chunk), :] = real[start : start + chunk]
                outs[at][shard, pl.ds(base + (2 + band) * chunk, chunk), :] = imag[start : start + chunk]
        columns = jnp.where(lane == band, pltpu.roll(cos_im, band, 1) if band else cos_im, columns)
        columns = jnp.where(lane == band + 2, -pltpu.roll(sin_im, band + 2, 1), columns)
    turned = columns.T[:8]
    slot = lax.broadcasted_iota(jnp.int32, (1, LANES), 1)
    for shard in range(plan.shards):
        start = shard * rows
        piece = turned[:, start // LANES * LANES : start // LANES * LANES + LANES]
        row = jnp.zeros((1, LANES), jnp.float32)
        for group in range(4):
            shift = (group * rows - start) % LANES
            held = pltpu.roll(piece, shift, 1) if shift else piece
            row = jnp.where((slot >= group * rows) & (slot < (group + 1) * rows), held[group : group + 1], row)
        outs[0][shard, pl.ds(plan.edge + cell, 1), :] = row


def inverse_slabs(plan, step, ins, beside, back, take):
    width = plan.width
    uppers, lowers = [], []
    for sub in range(plan.batch):
        inverse_cell(plan, step * plan.batch + sub, sub, ins, uppers, lowers)
    pairs = jnp.concatenate([jnp.concatenate(uppers, axis=1), jnp.concatenate(lowers, axis=1)], axis=0)
    mixed = dot3(beside, split(pairs))
    slabs = [mixed[:, i * width : (i + 1) * width] for i in range(2 * plan.batch)]
    out = dot3(split(jnp.concatenate(slabs, axis=0)), back)
    for sub in range(plan.batch):
        for band in range(2):
            start = (2 * sub + band) * width
            take(sub, band, out[start : start + width])


def inverse_cell(plan, cell, sub, ins, uppers, lowers):
    width, half, rows, chunk = plan.width, plan.half, plan.rows, plan.chunk
    lines = [ins[0][shard, pl.ds(plan.edge + cell, 1), :] for shard in range(plan.shards)]
    lines.append(jnp.zeros((LANES - plan.shards, LANES), jnp.float32))
    turned = jnp.concatenate(lines, axis=0).T[: 4 * rows]
    shifted = [pltpu.roll(turned, LANES - shard, 1) if shard else turned for shard in range(plan.shards)]
    sides = [jnp.concatenate([held[g * rows : (g + 1) * rows] for held in shifted], axis=0) for g in range(4)]
    first = lax.broadcasted_iota(jnp.int32, (width, half), 1) == 0
    for band in range(2):
        reals, imags = [], []
        for shard in range(plan.shards):
            for at in range(plan.chunks):
                base = pl.multiple_of(cell * plan.main, 8) if at == 0 else sub * plan.main
                reals.append(ins[at][shard, pl.ds(base + band * chunk, chunk), :])
                imags.append(ins[at][shard, pl.ds(base + (2 + band) * chunk, chunk), :])
        real, imag = jnp.concatenate(reals, axis=0), jnp.concatenate(imags, axis=0)
        uppers += [real, jnp.where(first, sides[band], imag)]
        lowers += [-imag, jnp.where(first, -sides[band + 2], real)]


def first_kernel(plan, kept, phi, into_h, into_l, stacked_h, stacked_l, *refs):
    cell = pl.program_id(0)
    outs = refs[kept:]
    into, stacked = (into_h[...], into_l[...]), (stacked_h[...], stacked_l[...])
    forward_slabs(plan, cell, lambda sub, band: phi[sub, band], into, stacked, outs)


def middle_kernel(plan, kept, *refs):
    cell = pl.program_id(0)
    ins = refs[: plan.chunks]
    coeff = refs[plan.chunks]
    into_h, into_l, stacked_h, stacked_l, beside_h, beside_l, back_h, back_l = refs[plan.chunks + 1 : plan.chunks + 9]
    outs, held = refs[plan.chunks + 9 + kept : -1], refs[-1]

    def take(sub, band, value):
        held[sub, band] = value * coeff[sub]

    inverse_slabs(plan, cell, ins, (beside_h[...], beside_l[...]), (back_h[...], back_l[...]), take)
    into, stacked = (into_h[...], into_l[...]), (stacked_h[...], stacked_l[...])
    forward_slabs(plan, cell, lambda sub, band: held[sub, band], into, stacked, outs)


def last_kernel(plan, *refs):
    ins = refs[: plan.chunks]
    coeff, beside_h, beside_l, back_h, back_l = refs[plan.chunks : plan.chunks + 5]
    out = refs[-1]

    def take(sub, band, value):
        out[sub, band] = value * coeff[sub]

    inverse_slabs(plan, pl.program_id(0), ins, (beside_h[...], beside_l[...]), (back_h[...], back_l[...]), take)


def whole(array):
    rank = len(array.shape)
    return pl.BlockSpec(array.shape, lambda cell: (0,) * rank)


def piece_specs(plan, side, sides):
    specs = []
    for at in range(plan.chunks):
        merged = sides(at) == 1
        if at == 0:
            shape = (plan.shards, plan.height(0), LANES)
            specs.append(pl.BlockSpec(shape, lambda cell, first=side if merged else 0: (0, first, 0)))
        else:
            shape = (plan.shards, plan.batch * plan.main, LANES)
            first = side * plan.cells // plan.batch if merged else 0
            specs.append(pl.BlockSpec(shape, lambda cell, first=first: (0, first + cell, 0)))
    return specs


def sent_shapes(plan):
    return [plan.shapes(at, plan.sides_sent(at))[0] for at in range(plan.chunks)]


def slab_spec(plan, side):
    return pl.BlockSpec((plan.batch, 2, plan.width, plan.width), lambda cell: (cell, side, 0, 0))


def coeff_spec(plan):
    return pl.BlockSpec((plan.batch, plan.width, plan.width), lambda cell: (cell, 0, 0))


def cost(microseconds):
    return pl.CostEstimate(flops=0, bytes_accessed=int(microseconds * 3.69e6), transcendentals=0)


PARAMS = pltpu.CompilerParams(vmem_limit_bytes=VMEM)


def send(kernel, plan, side, operands, in_specs, held, microseconds, scratch, name):
    aliases = {}
    for at in range(plan.chunks):
        if held is not None and plan.sides_sent(at) == 1:
            aliases[len(operands)] = at
            operands, in_specs = operands + [held[at]], in_specs + [pl.BlockSpec(memory_space=pl.ANY)]
    return pl.pallas_call(
        functools.partial(kernel, plan, len(aliases)),
        grid=(plan.cells // plan.batch,),
        in_specs=in_specs,
        out_specs=piece_specs(plan, side, plan.sides_sent),
        out_shape=sent_shapes(plan),
        input_output_aliases=aliases,
        scratch_shapes=scratch,
        compiler_params=PARAMS,
        cost_estimate=cost(microseconds),
        name=name,
    )(*operands)


def first(plan, side, phi, consts, held):
    in_specs = [slab_spec(plan, side)] + [whole(c) for c in consts[:4]]
    return send(first_kernel, plan, side, [phi, *consts[:4]], in_specs, held, 12, [], "into_modes")


def middle(plan, side, ins, coeff, consts, held):
    in_specs = piece_specs(plan, side, plan.sides_back) + [coeff_spec(plan)] + [whole(c) for c in consts]
    scratch = [pltpu.VMEM((plan.batch, 2, plan.width, plan.width), jnp.float32)]
    return send(middle_kernel, plan, side, [*ins, coeff, *consts], in_specs, held, 25, scratch, "between_steps")


def last(plan, side, ins, coeff, consts, held):
    operands = [*ins, coeff, *consts[4:]]
    in_specs = piece_specs(plan, side, plan.sides_back) + [coeff_spec(plan)] + [whole(c) for c in consts[4:]]
    aliases = {}
    if held is not None:
        aliases = {len(operands): 0}
        operands.append(held)
        in_specs.append(pl.BlockSpec(memory_space=pl.ANY))
    return pl.pallas_call(
        functools.partial(last_kernel, plan),
        grid=(plan.cells // plan.batch,),
        in_specs=in_specs,
        out_specs=slab_spec(plan, side),
        out_shape=jax.ShapeDtypeStruct((plan.cells, 4, plan.width, plan.width), jnp.float32),
        input_output_aliases=aliases,
        compiler_params=PARAMS,
        cost_estimate=cost(16),
        name="out_of_modes",
    )(*operands)


def sweep_kernel(plan, at, upward, groups, *refs):
    refs = list(refs)

    def pop(count):
        taken = refs[:count]
        del refs[:count]
        return taken

    specs = views(plan, at, pop(plan.sides_sent(at)))
    aims, inv, couple, rate = pop(4)
    if upward:
        parts = views(plan, at, pop(2))
        extras = pop(1)[0] if at == 0 else None
        share, keep = pop(2)
        fluxes = pop(groups)
        outs = views(plan, at, pop(plan.sides_back(at)))
        sums, totals = refs
    else:
        outs = views(plan, at, pop(2))
        flux, sums = pop(2)
        extras = pop(1)[0] if at == 0 else None
        totals = refs[0]
    tiles, depth, cells, main, rows = plan.tiles, plan.depth, plan.cells, plan.main, plan.rows
    imag_at = 2 * plan.chunk
    sub = lax.broadcasted_iota(jnp.int32, (8, LANES), 0)
    lane = lax.broadcasted_iota(jnp.int32, (1, LANES), 1)
    zeros = jnp.zeros((8, LANES), jnp.float32)
    cosine = [abs(float(c)) / 12.0 for c in quadrature()[0][:6]]

    def place(cell, base, tile):
        return pl.ds(cell * main + base + tile, 8, stride=tiles)

    def extra_source(shard, cell, base):
        edge = []
        for s in range(2):
            line = specs[s].at(shard, pl.ds(plan.edge + cell, 1))
            line = pltpu.roll(line, LANES - 2 * rows, 1) if base else line
            edge.append(jnp.where(sub < 4, line, pltpu.roll(line, LANES - rows, 1)))
        row0 = [specs[s].at(shard, place(cell, base, 0)) for s in range(2)]
        kind = sub % 4
        value = jnp.where(kind == 0, row0[0], jnp.where(kind == 1, pltpu.roll(row0[1], 1, 0), 0.0))
        return jnp.where(kind == 2, edge[0], jnp.where(kind == 3, edge[1], value))

    def extra_store(shard, cell, new_re, new_im):
        if not upward:
            extras[shard * cells + cell, 0] = new_re
            extras[shard * cells + cell, 1] = new_im
            return
        new_re = new_re + extras[shard * cells + cell, 0]
        new_im = new_im + extras[shard * cells + cell, 1]
        spread = [new_re, pltpu.roll(new_re, rows, 1), pltpu.roll(new_im, 2 * rows, 1), pltpu.roll(new_im, 3 * rows, 1)]
        for side in range(2):
            row = spread[0][2 + side : 3 + side]
            for group in range(1, 4):
                at_sub = 2 + side + 4 * (group % 2)
                row = jnp.where(lane < group * rows, row, spread[group][at_sub : at_sub + 1])
            outs[side].put(shard, pl.ds(plan.edge + cell, 1), row)
            for base, value in ((0, new_re), (imag_at, new_im)):
                value = pltpu.roll(value, 7, 0) if side else value
                held = outs[side].at(shard, place(cell, base, 0))
                pair = (sub % 4 == 0) & (keep[...] > 0.0)
                outs[side].put(shard, place(cell, base, 0), jnp.where(pair, 0.5 * (held + value), held))

    for count in range(2 * tiles + (1 if at == 0 else 0)):
        extra = count == 2 * tiles
        side, tile = (2, tiles) if extra else (count // tiles, count % tiles)
        inv_re = [inv[0, d, count] for d in range(6)]
        inv_im = [inv[1, d, count] for d in range(6)]
        fresh = extra or tile == 0

        def block(step, psi, extra=extra, side=side, tile=tile, inv_re=inv_re, inv_im=inv_im, fresh=fresh):
            psi_re, psi_im = list(psi[:6]), list(psi[6:])
            shard = step if upward else plan.shards - 1 - step
            for cell in range(cells) if upward else range(cells - 1, -1, -1):
                z = shard * cells + cell
                if extra:
                    row_re, row_im = extra_source(shard, cell, 0), extra_source(shard, cell, imag_at)
                else:
                    row_re = specs[side].at(shard, place(cell, 0, tile))
                    row_im = specs[side].at(shard, place(cell, imag_at, tile))
                row_re, row_im = rate[side] * row_re, rate[side] * row_im
                aim_re, aim_im = aims[z, 0, tile], aims[z, 1, tile]
                for d in range(6):
                    sum_re = row_re + couple[side, d] * psi_re[d]
                    sum_im = row_im + couple[side, d] * psi_im[d]
                    psi_re[d] = inv_re[d] * sum_re - inv_im[d] * sum_im
                    psi_im[d] = inv_re[d] * sum_im + inv_im[d] * sum_re
                    product = psi_re[d] * aim_re + psi_im[d] * aim_im
                    totals[side, d, z] = product if fresh else totals[side, d, z] + product
                new_re = ((psi_re[0] + psi_re[1]) + (psi_re[2] + psi_re[3])) + (psi_re[4] + psi_re[5])
                new_im = ((psi_im[0] + psi_im[1]) + (psi_im[2] + psi_im[3])) + (psi_im[4] + psi_im[5])
                if extra:
                    extra_store(shard, cell, new_re, new_im)
                    continue
                if upward:
                    new_re = new_re + parts[side].at(shard, place(cell, 0, tile))
                    new_im = new_im + parts[side].at(shard, place(cell, imag_at, tile))
                outs[side].put(shard, place(cell, 0, tile), new_re)
                outs[side].put(shard, place(cell, imag_at, tile), new_im)
            return tuple(psi_re + psi_im)

        if upward:
            start = []
            for part in range(2):
                value = fluxes[0][part, tile]
                for other in fluxes[1:]:
                    value = value + other[part, tile]
                start += [share[side] * value] * 6
        else:
            start = [zeros] * 12
        carried = lax.fori_loop(0, plan.shards, block, tuple(start))
        if not upward:
            for part in range(2):
                value = carried[6 * part] * cosine[0]
                for d in range(1, 6):
                    value = value + carried[6 * part + d] * cosine[d]
                value = value + pltpu.roll(value, 4, 0)
                if extra:
                    swapped = jnp.where(sub % 2 == 0, pltpu.roll(value, 7, 0), pltpu.roll(value, 1, 0))
                    flux[part, tile] = value + swapped
                elif side == 0:
                    flux[part, tile] = value
                else:
                    flux[part, tile] = flux[part, tile] + value
    for side in range(3 if at == 0 else 2):
        for d in range(6):
            sums[side, d] = jnp.sum(totals[side, d], axis=-1)


def sweep(plan, at, upward, groups, *operands):
    tiles = plan.steps(at)
    sides = 3 if at == 0 else 2
    vmem = pl.BlockSpec(memory_space=pltpu.VMEM)
    out_shape = plan.shapes(at, plan.sides_back(at) if upward else 2)
    if not upward:
        out_shape.append(jax.ShapeDtypeStruct((2, tiles, 8, LANES), jnp.float32))
    out_shape.append(jax.ShapeDtypeStruct((sides, 6, plan.depth, 8), jnp.float32))
    if not upward and at == 0:
        out_shape.append(jax.ShapeDtypeStruct((plan.depth, 2, 8, LANES), jnp.float32))
    return pl.pallas_call(
        functools.partial(sweep_kernel, plan, at, upward, groups),
        in_specs=[vmem] * len(operands),
        out_specs=[vmem] * len(out_shape),
        out_shape=out_shape,
        scratch_shapes=[pltpu.VMEM((sides, 6, plan.depth, 8, LANES), jnp.float32)],
        compiler_params=PARAMS,
        cost_estimate=cost(13),
        name="upward" if upward else "downward",
    )(*operands)


def mirror_kernel(plan, group, upper, lanes_turned, rows_turned, turned, lead):
    rows, half = plan.rows, plan.half
    cells = rows_turned.shape[0] // rows
    for part in range(2):
        sign = 1.0 if part == 0 else -1.0
        for at in range(0, upper.shape[1], cells):
            pairs = split(sign * upper[part, at : at + cells].reshape(cells * rows, half))
            value = dot(pairs[0], lanes_turned[...]) + dot(pairs[1], lanes_turned[...])
            lead[part, at : at + cells] = value.reshape(cells, rows, half)[:, 0, :]
            pairs = split(value)
            value = dot(rows_turned[...], pairs[0]) + dot(rows_turned[...], pairs[1])
            turned[part, at : at + cells] = value.reshape(cells, rows, half)


def mirror(plan, forward, groups):
    cells = 8
    rows, half = plan.rows, plan.half
    share = plan.depth // groups
    lanes_turned = np.zeros((half, half), ml_dtypes.bfloat16)
    rows_turned = np.zeros((cells * rows, cells * rows), ml_dtypes.bfloat16)
    for k in range(1, half):
        lanes_turned[half - k, k] = 1
    for c in range(cells):
        for r in range(1, rows):
            rows_turned[c * rows + r, c * rows + rows - r] = 1
    lanes_turned, rows_turned = jnp.asarray(lanes_turned), jnp.asarray(rows_turned)
    group = lax.axis_index("ba").astype(jnp.int32).reshape(1)
    spec = pltpu.PrefetchScalarGridSpec(
        num_scalar_prefetch=1,
        grid=(forward.shape[0],),
        in_specs=[
            pl.BlockSpec((None, 2, share, rows, half), lambda step, at: (step, 0, at[0], 0, 1)),
            pl.BlockSpec(lanes_turned.shape, lambda step, at: (0, 0)),
            pl.BlockSpec(rows_turned.shape, lambda step, at: (0, 0)),
        ],
        out_specs=[
            pl.BlockSpec((None, 2, share, rows, half), lambda step, at: (step, 0, 0, 0, 0)),
            pl.BlockSpec((None, 2, share, half), lambda step, at: (step, 0, 0, 0)),
        ],
    )
    return pl.pallas_call(
        functools.partial(mirror_kernel, plan),
        grid_spec=spec,
        out_shape=[
            jax.ShapeDtypeStruct((forward.shape[0], 2, share, rows, half), jnp.float32),
            jax.ShapeDtypeStruct((forward.shape[0], 2, share, half), jnp.float32),
        ],
        compiler_params=PARAMS,
        cost_estimate=cost(5),
        name="mirrored",
    )(group, forward, lanes_turned, rows_turned)


def aims_kernel(plan, at, group, own, other, keep, out, held):
    half, chunk, tiles = plan.half, plan.chunk, plan.tiles
    cells, rows = own.shape[1:3]
    row = lax.broadcasted_iota(jnp.int32, (chunk, half), 0)
    sub = lax.broadcasted_iota(jnp.int32, (8, LANES), 0)
    lane = lax.broadcasted_iota(jnp.int32, (1, LANES), 1)
    for part in range(2):
        if at == 0:
            owner = keep[...] > 0.0
            line = own[part, :, :, half:].reshape(cells * rows, half).T[:1]
            if cells * rows < LANES:
                line = jnp.concatenate([line, jnp.zeros((1, LANES - cells * rows), jnp.float32)], axis=1)
        for cell in range(cells):
            mine, theirs = own[part, cell, :chunk, :half], other[part, cell]
            if at == 0:
                held[...] = mine + jnp.where((row == 0) & owner[:1], 0.0, theirs)
            else:
                held[...] = mine + theirs
            for tile in range(tiles):
                four = held[pl.ds(tile, 4, stride=tiles), :]
                out[cell, part, tile] = jnp.concatenate([four, four], axis=0)
            if at == 0:
                partner = jnp.where(owner, theirs[:1], 0.0)
                start = cell * rows
                piece = line[:, start // LANES * LANES : start // LANES * LANES + LANES]
                at_zero = pltpu.roll(piece, LANES - start % LANES, 1) if start % LANES else piece
                out[cell, part, tiles] = jnp.where(sub % 4 < 2, partner, jnp.where(lane < rows, at_zero, 0.0))


def make_aims(plan, at, own, parts, keep, step):
    cells = 8
    half, chunk = plan.half, plan.chunk
    other = jnp.stack(parts)
    groups = other.shape[0]
    blocks = other.shape[2] // cells
    group = lax.axis_index("ba").astype(jnp.int32).reshape(1)
    own_rows = plan.rows if at == 0 else chunk

    def sender(z, me):
        return (lax.rem(me[0] + groups - z // blocks, groups), 0, z % blocks, 0, 0)

    spec = pltpu.PrefetchScalarGridSpec(
        num_scalar_prefetch=1,
        grid=(plan.depth // cells,),
        in_specs=[
            pl.BlockSpec((None, 2, cells, own_rows, plan.width), lambda z, me: (step, 0, z, at, 0)),
            pl.BlockSpec((None, 2, cells, chunk, half), sender),
            pl.BlockSpec(keep.shape, lambda z, me: (0, 0)),
        ],
        out_specs=pl.BlockSpec((cells, 2, plan.steps(at), 8, LANES), lambda z, me: (z, 0, 0, 0, 0)),
        scratch_shapes=[pltpu.VMEM((chunk, half), jnp.float32)],
    )
    return pl.pallas_call(
        functools.partial(aims_kernel, plan, at),
        grid_spec=spec,
        out_shape=jax.ShapeDtypeStruct((plan.depth, 2, plan.steps(at), 8, LANES), jnp.float32),
        compiler_params=PARAMS,
        cost_estimate=cost(4),
        name="targets",
    )(group, own, other, keep)


def lift(value):
    main = jnp.broadcast_to(value.reshape(2, 2, 1), (2, 2, 4)).reshape(2, 8)
    extra = jnp.broadcast_to(value.reshape(2, 2).T[:, None, :], (2, 2, 2)).reshape(1, 8)
    return jnp.broadcast_to(jnp.concatenate([main, extra])[:, :, None], (3, 8, LANES))


def factors(plan, at, place, rate, speed):
    unit = 1.5 * 2.0 * math.pi / plan.width
    half, width, tiles = plan.half, plan.width, plan.tiles
    base = place * plan.rows
    sub = jnp.arange(8)

    def signed(index):
        return ((index + half) % width - half).astype(jnp.float32) * unit

    row = base + at * plan.chunk + jnp.arange(tiles)[:, None] + tiles * (sub % 4)[None, :]
    freq_x = jnp.broadcast_to(signed(row)[None, :, :, None], (2, tiles, 8, LANES)).reshape(2 * tiles, 8, LANES)
    freq_y = jnp.broadcast_to(signed(jnp.arange(LANES)), (2 * tiles, 8, LANES))
    sides = [0] * tiles + [1] * tiles
    if at == 0:
        partner = (sub % 4 < 2)[:, None]
        extra_x = jnp.where(partner, -signed(base), signed(base + jnp.arange(LANES) % plan.rows)[None, :])
        extra_y = jnp.where(partner, signed(jnp.arange(LANES))[None, :], signed(jnp.asarray(half)))
        freq_x = jnp.concatenate([freq_x, extra_x[None]], axis=0)
        freq_y = jnp.concatenate([freq_y, extra_y[None]], axis=0)
        sides.append(2)
    rate, speed = [jnp.concatenate([v[s : s + 1] for s in sides]) for v in (rate, speed)]
    cosine, along_x, along_y = [np.asarray(q, np.float32).reshape(12, 1, 1, 1) for q in quadrature()]
    wave = speed * (along_x * freq_x + along_y * freq_y)
    real = rate + np.abs(cosine) * speed
    denom = real * real + wave * wave
    return jnp.stack([real / denom, -wave / denom])


def body(phi_start, coeff, forward, rates, speeds, shares):
    shards = lax.axis_size("gx")
    groups = lax.axis_size("ba")
    place = lax.axis_index("gx")
    cells, bands, width, _ = phi_start.shape
    rows = forward.shape[3]
    steps = forward.shape[0]
    plan = Plan(shards, cells, width, rows)
    wide = Plan(shards, cells, width, rows, 2 if cells % 2 == 0 else 1)
    depth = plan.depth
    consts = [jnp.asarray(part) for part in tables(width)]
    owner = place * rows == plan.half
    keep = jnp.broadcast_to(jnp.where(owner, 1.0, 0.0).astype(jnp.float32), (8, LANES))
    rate, speed, share = lift(rates), lift(speeds), lift(shares)
    polar = np.abs(np.asarray(quadrature()[0][:6], np.float32)).reshape(1, 6, 1, 1)
    couple = polar * speed[:, None]
    inverse = [factors(plan, at, place, rate, speed) for at in range(plan.chunks)]

    def tie(value, *others):
        return lax.optimization_barrier((value, *others))[0]

    def swap_targets(turned, lead):
        turned = lax.ppermute(turned, "gx", [(i, shards - 1 - i) for i in range(shards)])
        lead = lax.ppermute(lead, "gx", [(i, (shards - i) % shards) for i in range(shards)])
        return jnp.where(jnp.arange(rows)[:, None] == 0, lead[:, :, :, None, :], turned)

    def spread_targets(turned):
        parts = [turned]
        for shift in range(1, groups):
            parts.append(lax.ppermute(turned, "ba", [(i, (i + shift) % groups) for i in range(groups)]))
        return parts

    def exchange(array):
        return lax.all_to_all(array, "gx", split_axis=0, concat_axis=0, tiled=True)

    main_sums, extra_sums = [[], []], [[], []]

    def collect(sums, way):
        main_sums[way].append(sums[:2])
        if sums.shape[0] == 3:
            extra_sums[way].append(sums[2])

    def into(transform):
        pieces, held = [[] for _ in range(plan.chunks)], None
        for side in range(2):
            held = transform(side, held)
            for at in range(plan.chunks):
                if plan.sides_sent(at) == 2 or side == 1:
                    pieces[at].append(held[at])
        return pieces

    def in_order(pieces, after, besides=()):
        arrived = []
        for piece in pieces:
            if after is not None:
                piece = tie(piece, after, *besides)
            after = exchange(piece)
            arrived.append(after)
        return arrived

    flipped = mirror(plan, forward, groups)
    swapped = swap_targets(*flipped)
    starts = [tie(phi_start, *flipped), tie(phi_start, swapped)]
    sent = into(lambda side, held: first(plan, side, starts[side], consts, held))
    chunk_rows = [slice(at * plan.chunk, (at + 1) * plan.chunk) for at in range(plan.chunks)]
    spread = [[spread_targets(swapped[step][:, :, held]) for held in chunk_rows] for step in range(steps)]
    early = make_aims(plan, 0, forward, spread[0][0], keep, 0)
    for step in range(steps):
        modes, after = [], None
        for at in range(plan.chunks):
            besides = ()
            if step == 0:
                besides = spread[0][at]
                if at == 1:
                    besides = [*besides, early]
            modes.append(in_order(sent[at], after, besides))
            after = modes[at][-1]
        back = []
        back = []
        for at in range(plan.chunks):
            inv = inverse[at]
            aims = early if step == 0 and at == 0 else make_aims(plan, at, forward, spread[step][at], keep, step)
            common = (*modes[at], aims)
            part0, part1, flux, sums, *extras = sweep(plan, at, False, groups, *common, inv[:, :6], couple, rate)
            collect(sums, 0)
            fluxes = [flux]
            for shift in range(1, groups):
                fluxes.append(lax.ppermute(flux, "ba", [(i, (i + shift) % groups) for i in range(groups)]))
            rest = (part0, part1, *extras, share, keep, *fluxes)
            *new, sums = sweep(plan, at, True, groups, *common, inv[:, 6:], couple, rate, *rest)
            collect(sums, 1)
            if step + 1 < steps and at == plan.chunks - 1:
                for part, parts in enumerate(spread[step + 1]):
                    new[part % len(new)] = tie(new[part % len(new)], *parts)
            back.append(in_order(new, back[-1][-1] if back else None))
        ends = [[pieces[side % len(pieces)] for pieces in back] for side in range(2)]
        if step + 1 < steps:
            sent = into(lambda side, held: middle(plan, side, ends[side], coeff, consts, held))
        else:
            upper = last(wide, 0, ends[0], coeff, consts, None)
            phi = last(wide, 1, ends[1], coeff, consts, upper)

    grads = []
    for way in range(2):
        main = sum(main_sums[way]).reshape(2, 6, depth, 2, 4).sum(axis=4)
        extra = sum(extra_sums[way]).reshape(6, depth, 2, 2, 2).sum(axis=3)
        grads.append(main.transpose(2, 1, 0, 3) + extra.transpose(1, 0, 3, 2))
    sums = jnp.stack(grads, axis=1).reshape(shards, cells * 12 * bands) * (1.0 / width)
    grad = exchange(tie(sums, back[-1][-1], upper)).sum(axis=0).reshape(cells, 12, bands)
    return (phi, grad)


def solution(mesh):
    in_specs = (
        P("gx", "ba", None, None),
        P("gx", None, None),
        P(None, None, None, "gx", None),
        P("ba"),
        P("ba"),
        P("ba"),
    )
    out_specs = (P("gx", "ba", None, None), P("gx", None, "ba"))
    return jax.shard_map(body, mesh=mesh, in_specs=in_specs, out_specs=out_specs, check_vma=False)
```
